512 devices in a mesh: row: 32 (over x_hi, z, core), col: 16 (over y, x_lo).
Axes of the slice: x: 4 (x_hi: 2, x_lo: 2; x = x_hi * 2 + x_lo), y: 8, z: 8, core: 2. Of those that a mesh axis runs over, the one named last changes fastest.
Arguments:
- normed: bfloat16 [65536, 8192], P(('row', 'col')), may hold values from -24 to 24
- norm_gain: float32 [8192], replicated, may hold values from 0.5 to 1.5
- kv_cot: bfloat16 [65536, 256], P(('row', 'col')), may hold values from -6 to 6
- master: float32 [8192, 256], P(('row', 'col')), may hold values from -0.0625 to 0.0625
- moment1: float32 [8192, 256], P(('row', 'col')), may hold values from -6 to 6
- moment2: float32 [8192, 256], P(('row', 'col')), may hold values from 0.1 to 4
Outputs:
- new_master: float32 [8192, 256], P(('row', 'col'))
- new_moment1: float32 [8192, 256], P(('row', 'col'))
- new_moment2: float32 [8192, 256], P(('row', 'col'))
- gain_grad: float32 [8192], replicated
- normed_grad: bfloat16 [65536, 8192], P(('row', 'col'))
The draws below stay inside these ranges and needn't reach their ends.
All inputs are finite; a program needn't handle non-finite values.
Results may differ from the reference program's by a relative error of at most 0.014.
Values may be sent and summed in bfloat16 or wider, within the bound.
A program may use at most 64 MiB of HBM per device.

```python
import math
import jax
import jax.numpy as jnp
from jax import lax

D = 8192
TOK_DEV = 128
STEP = 100
KVW = 256
TOKENS = 65536
N_ROW = 32
N_COL = 16


def with_spikes(drawn, own_key, source, target, shards_of, factor):
    def block_of(dim):
        return (jnp.arange(drawn.shape[dim]) // (drawn.shape[dim] // shards_of)).reshape((-1,) + (1,) * (drawn.ndim - 1 - dim))

    first = jax.random.permutation(own_key, shards_of)[block_of(target)]
    second = (block_of(target) + shards_of // 2) % shards_of
    return jnp.where((block_of(source) == first) | (block_of(source) == second), factor * drawn, drawn)


def block_levels(rng, shape, pieces, low, high):
    loudness, own = 1.0, jax.random.fold_in(rng, 6)
    for dim, blocks in pieces:
        draws = jnp.exp(jax.random.uniform(jax.random.fold_in(own, dim), (blocks,), jnp.float32, low / len(pieces), high / len(pieces)))
        loudness = loudness * jnp.repeat(draws, shape[dim] // blocks).reshape([-1 if axis == dim else 1 for axis in range(len(shape))])
    return loudness


def noise(stream_key, extent, width, reach, split=(), dtype=jnp.bfloat16):
    array = jax.random.normal(stream_key, extent, jnp.float32) * width
    if len(split) > 0:
        array = block_levels(stream_key, extent, split, -0.22, 0.18) * array
    return jnp.clip(array, min=-reach, max=reach).astype(dtype)


def bell_draw_with(rng, dims, deviation, limit, pieces, heavy, kind=jnp.bfloat16):
    entries = deviation * jax.random.normal(rng, dims, jnp.float32)
    if pieces:
        entries = entries * block_levels(rng, dims, pieces, -0.22, 0.18)
    return jnp.clip(with_spikes(entries, jax.random.fold_in(rng, 3), *heavy), -limit, limit).astype(kind)


def setup_inputs(seed: int = 0) -> dict:
    arg_keys = jax.random.split(jax.random.key(seed), 7)
    return {
        "normed": bell_draw_with(arg_keys[0], (TOKENS, D), 1.0, 24.0, ((0, 512),), (0, 1, 512, 6.0)),
        "norm_gain": jnp.clip(1.0 + 0.1 * jax.random.normal(arg_keys[1], (D,), jnp.float32), 0.5, 1.5),
        "kv_cot": noise(arg_keys[2], (TOKENS, KVW), 1.0, 6.0, ((0, 512),)),
        "master": noise(arg_keys[3], (D, KVW), D ** -0.5, 0.0625, ((0, 512),), jnp.float32),
        "moment1": noise(arg_keys[4], (D, KVW), 1.0, 6.0, ((0, 512),), jnp.float32),
        "moment2": jnp.clip(jnp.exp(math.log(4.0) - 3.6888794 * jax.random.uniform(arg_keys[5], (D, KVW), jnp.float32) ** block_levels(arg_keys[5], (D, KVW), ((0, 512),), -0.2, 0.2)), 0.1, 4.0),
    }


def reference(normed, norm_gain, kv_cot, master, moment1, moment2):
    scale = 1.0 / float(TOKENS) ** 0.5
    blocks_x = normed.reshape(N_ROW, N_COL, TOK_DEV, D)
    blocks_g = kv_cot.reshape(N_ROW, N_COL, TOK_DEV, KVW)
    weights16 = master.astype(jnp.bfloat16).astype(jnp.float32)

    def advance(carry, pair):
        gain_acc, total_sum = carry
        xb, gb = pair
        xf = xb.astype(jnp.float32)
        gf = gb.astype(jnp.float32)
        inputs = (xf * norm_gain).astype(jnp.bfloat16).astype(jnp.float32)
        input_grad = jnp.einsum('ctk,dk->ctd', gf, weights16)
        normed_block = (input_grad * norm_gain).astype(jnp.bfloat16)
        gain_acc = gain_acc + lax.optimization_barrier(jnp.sum(input_grad * xf, axis=(0, 1)))
        terms = jnp.einsum('ctd,ctk->cdk', inputs, gf).astype(jnp.bfloat16)
        terms = lax.optimization_barrier(terms).astype(jnp.float32)
        return ((gain_acc, total_sum + lax.optimization_barrier(jnp.sum(terms, axis=0))), normed_block)
    init = (jnp.zeros((D,), jnp.float32), jnp.zeros((D, KVW), jnp.float32))
    (gain_acc, total_sum), normed_blocks = lax.scan(advance, init, (blocks_x, blocks_g))
    normed_grad = normed_blocks.reshape(TOKENS, D)
    grad = total_sum * scale
    gain_grad = gain_acc * scale
    new_moment1 = 0.9 * moment1 + 0.1 * grad
    new_moment2 = 0.95 * moment2 + 0.05 * grad * grad
    first = new_moment1 / (1.0 - 0.9 ** STEP)
    second = new_moment2 / (1.0 - 0.95 ** STEP)
    new_master = master - 0.01 * (first / (jnp.sqrt(second) + 1e-08) + 0.1 * master)
    return (new_master, new_moment1, new_moment2, gain_grad, normed_grad)
```

```python
import jax
import jax.numpy as jnp
from jax import lax
from jax.experimental import pallas as pl
from jax.experimental.pallas import tpu as pltpu
from jax.sharding import PartitionSpec as P

STEP = 100
TOTAL_TOKENS = 65536
SCALE = 1.0 / float(TOTAL_TOKENS) ** 0.5
MESH = pl.DeviceIdType.MESH
F32 = jnp.float32
BF16 = jnp.bfloat16

AG0_A, AG1_B, AG0_B, AG1_X, AG0_X, AG1_A = 0, 1, 2, 3, 4, 5
RS0_X, RS1_A, RS0_B, RS1_X, RS0_A, RS1_B = 6, 7, 8, 9, 10, 11
GAIN_A, GAIN_B, GAIN_X, GAIN_C = 12, 13, 14, 15
STAGES = 16
BLOCKS = 16


def kernel(
    normed, gain, kv, master, moment1, moment2,
    new_master, new_moment1, new_moment2, gain_grad, normed_grad,
    xb, kv2, w, g, rx0, s0, rb0, t0, ra0, ra1, s1, rx1, t1, rb1,
    ga, gb, gx, gsum, gsib, stage,
    ssem, rsem, ex_send, ex_recv, ex_local, out_send, out_recv, out_local,
):
    r = lax.axis_index("row")
    c = lax.axis_index("col")
    core = lax.rem(r, 2)
    z = lax.rem(lax.div(r, 2), 8)
    xh = lax.div(r, 16)
    xl = lax.rem(c, 2)
    y = lax.div(c, 2)
    x = xh * 2 + xl
    a = z * (1 - core) + y * core
    b = y * (1 - core) + z * core

    def dev(xx, aa, bb, cc=None):
        zz = aa * (1 - core) + bb * core
        yy = bb * (1 - core) + aa * core
        cc = core if cc is None else cc
        return {"row": lax.div(xx, 2) * 16 + zz * 2 + cc, "col": yy * 2 + lax.rem(xx, 2)}

    sibling = dev(x, a, b, 1 - core)
    x_peer = [lax.rem(x + k, 4) for k in range(1, 4)]
    a_peer = [lax.rem(a + k, 8) for k in range(1, 8)]
    b_peer = [lax.rem(b + k, 8) for k in range(1, 8)]
    x_dev = [dev(v, a, b) for v in x_peer]
    a_dev = [dev(x, v, b) for v in a_peer]
    b_dev = [dev(x, a, v) for v in b_peer]

    def cols(j, cc):
        return pl.ds(pl.multiple_of(j * 512 + cc * 256, 256), 256)

    own_rows = pl.ds(pl.multiple_of(core * 128, 128), 128)
    sib_rows = pl.ds(pl.multiple_of((1 - core) * 128, 128), 128)

    def remote(src, dst, send, recv, device):
        return pltpu.make_async_remote_copy(
            src_ref=src, dst_ref=dst, send_sem=send, recv_sem=recv,
            device_id=device, device_id_type=MESH,
        )

    def exchange(stage_no, devices, srcs, dsts):
        made = [
            remote(srcs[k], dsts[k], ssem.at[stage_no, k], rsem.at[stage_no, k], devices[k])
            for k in range(len(devices))
        ]
        for copy in made:
            copy.start()
        return made

    def arrive(made):
        for copy in made:
            copy.wait_recv()

    def load_copy(j):
        return pltpu.make_async_copy(normed.at[:, cols(j, core)], xb.at[j, own_rows], ex_local.at[j])

    def swap_copy(j):
        return remote(
            normed.at[:, cols(j, 1 - core)], xb.at[j, own_rows], ex_send.at[j], ex_recv.at[j], sibling
        )

    kv_load = pltpu.make_async_copy(kv, kv2.at[own_rows], ex_local.at[BLOCKS])
    kv_swap = remote(kv, kv2.at[own_rows], ex_send.at[BLOCKS], ex_recv.at[BLOCKS], sibling)

    kv_load.start()

    @pl.loop(0, BLOCKS)
    def _(j):
        load_copy(j).start()

    w[0, xh, a, b, xl] = master[:, :128].astype(BF16)
    w[1, xh, a, b, xl] = master[:, 128:].astype(BF16)

    barrier = pltpu.get_barrier_semaphore()
    partners = [sibling] + x_dev + a_dev + b_dev
    for device in partners:
        pl.semaphore_signal(barrier, inc=1, device_id=device, device_id_type=MESH)
    pl.semaphore_wait(barrier, len(partners))

    first0 = w.at[0, xh, a, b, xl]
    first1 = w.at[1, xh, a, b, xl]
    ag0_a = exchange(AG0_A, a_dev, [first0] * 7, [first0] * 7)
    ag1_b = exchange(AG1_B, b_dev, [first1] * 7, [first1] * 7)

    kv_swap.start()

    @pl.loop(0, BLOCKS)
    def _(j):
        swap_copy(j).start()

    arrive(ag0_a)
    line0 = w.at[0, xh, :, b, xl]
    ag0_b = exchange(AG0_B, b_dev, [line0] * 7, [line0] * 7)
    arrive(ag1_b)
    line1 = w.at[1, xh, a, :, xl]
    ag1_x = exchange(AG1_X, x_dev, [line1] * 3, [line1] * 3)

    kv_load.wait()
    kv_swap.wait_recv()

    @pl.loop(0, BLOCKS)
    def _(j):
        load_copy(j).wait()
        swap_copy(j).wait_recv()
        term = lax.dot_general(
            xb[j], kv2[...], (((0,), (0,)), ((), ())), preferred_element_type=F32
        ).astype(BF16)
        bh = lax.div(j, 8)
        bz = lax.rem(j, 8)
        for i in range(8):
            ia = bz * (1 - core) + i * core
            ib = i * (1 - core) + bz * core
            piece = term[32 * i : 32 * i + 32]
            g[0, bh, ia, ib] = piece[:, :128].reshape(2, 16, 128)
            g[1, bh, ia, ib] = piece[:, 128:].reshape(2, 16, 128)

    arrive(ag1_x)
    plane1 = w.at[1, :, a]
    ag1_a = exchange(AG1_A, a_dev, [plane1] * 7, [plane1] * 7)
    arrive(ag0_b)
    plane0 = w.at[0, xh, :, :, xl]
    ag0_x = exchange(AG0_X, x_dev, [plane0] * 3, [plane0] * 3)
    rs0_x = exchange(
        RS0_X, x_dev, [g.at[0, lax.div(v, 2), :, :, lax.rem(v, 2)] for v in x_peer], [rx0.at[k] for k in range(3)]
    )
    rs1_a = exchange(RS1_A, a_dev, [g.at[1, :, v] for v in a_peer], [ra1.at[k] for k in range(7)])

    arrive(ag1_a)
    arrive(ag0_x)

    def out_copy(j):
        return pltpu.make_async_copy(
            stage.at[j, own_rows], normed_grad.at[:, cols(j, core)], out_local.at[j]
        )

    def out_swap(j):
        return remote(
            stage.at[j, sib_rows], normed_grad.at[:, cols(j, core)], out_send.at[j], out_recv.at[j], sibling
        )

    @pl.loop(0, BLOCKS)
    def _(j):
        bh = lax.div(j, 8)
        bz = lax.rem(j, 8)
        pieces = []
        for i in range(8):
            ia = bz * (1 - core) + i * core
            ib = i * (1 - core) + bz * core
            pieces.append(
                jnp.concatenate(
                    [w[0, bh, ia, ib].reshape(32, 128), w[1, bh, ia, ib].reshape(32, 128)], axis=1
                )
            )
        block = jnp.concatenate(pieces, axis=0)
        input_grad = lax.dot_general(
            kv2[...], block, (((1,), (1,)), ((), ())), preferred_element_type=F32
        )
        row = 4 * j + 2 * core
        factor = jnp.concatenate([gain[pl.ds(row, 1), :], gain[pl.ds(row + 1, 1), :]], axis=1)
        stage[j] = (input_grad * factor).astype(BF16)
        out_copy(j).start()
        out_swap(j).start()
        part = jnp.sum(input_grad * xb[j].astype(F32), axis=0, keepdims=True)
        ga[a, pl.ds(2 * j, 1), :] = part[:, :128]
        ga[a, pl.ds(2 * j + 1, 1), :] = part[:, 128:]

    gain_a = exchange(GAIN_A, a_dev, [ga.at[a]] * 7, [ga.at[a]] * 7)

    arrive(rs0_x)

    @pl.loop(0, 8)
    def _(i):
        total = g[0, xh, i, :, xl].astype(F32)
        for k in range(3):
            total = total + rx0[k, i].astype(F32)
        s0[i] = total.astype(BF16)

    rs0_b = exchange(RS0_B, b_dev, [s0.at[:, v] for v in b_peer], [rb0.at[k] for k in range(7)])
    arrive(rs1_a)

    @pl.loop(0, 8)
    def _(i):
        for h in range(2):
            total = g[1, h, a, i].astype(F32)
            for k in range(7):
                total = total + ra1[k, h, i].astype(F32)
            s1[h, i] = total.astype(BF16)

    rs1_x = exchange(
        RS1_X, x_dev, [s1.at[lax.div(v, 2), :, lax.rem(v, 2)] for v in x_peer], [rx1.at[k] for k in range(3)]
    )

    def gain_total(ref, count):
        total = ref[0]
        for k in range(1, count):
            total = total + ref[k]
        return total

    arrive(gain_a)
    gb[b] = gain_total(ga, 8)
    gain_b = exchange(GAIN_B, b_dev, [gb.at[b]] * 7, [gb.at[b]] * 7)

    arrive(rs1_x)
    total = s1[xh, :, xl].astype(F32)
    for k in range(3):
        total = total + rx1[k].astype(F32)
    t1[...] = total.astype(BF16)
    rs1_b = exchange(RS1_B, b_dev, [t1.at[v] for v in b_peer], [rb1.at[k] for k in range(7)])
    arrive(rs0_b)
    total = s0[:, b].astype(F32)
    for k in range(7):
        total = total + rb0[k].astype(F32)
    t0[...] = total.astype(BF16)
    rs0_a = exchange(RS0_A, a_dev, [t0.at[v] for v in a_peer], [ra0.at[k] for k in range(7)])

    arrive(gain_b)
    gx[x] = gain_total(gb, 8)
    gain_x = exchange(GAIN_X, x_dev, [gx.at[x]] * 3, [gx.at[x]] * 3)

    arrive(rs1_b)
    total1 = t1[b].astype(F32)
    for k in range(7):
        total1 = total1 + rb1[k].astype(F32)
    arrive(rs0_a)
    total0 = t0[a].astype(F32)
    for k in range(7):
        total0 = total0 + ra0[k].astype(F32)

    arrive(gain_x)
    gsum[...] = gain_total(gx, 4) * SCALE
    gain_c = exchange(GAIN_C, [sibling], [gsum], [gsib])

    p = r * 16 + c
    own_gain = jnp.broadcast_to(gain[pl.ds(lax.div(p, 8), 1), :], (16, 128))
    lane = lax.broadcasted_iota(jnp.int32, (16, 128), 1)
    sub = lax.broadcasted_iota(jnp.int32, (16, 128), 0)
    factor = jnp.sum(
        jnp.where(lane == sub + lax.rem(p, 8) * 16, own_gain, 0.0), axis=1, keepdims=True
    )
    grad = jnp.concatenate([total0, total1], axis=1) * (factor * SCALE)
    m1 = 0.9 * moment1[...] + 0.1 * grad
    m2 = 0.95 * moment2[...] + 0.05 * grad * grad
    new_moment1[...] = m1
    new_moment2[...] = m2
    first = m1 / (1.0 - 0.9**STEP)
    second = m2 / (1.0 - 0.95**STEP)
    new_master[...] = master[...] - 0.01 * (first / (jnp.sqrt(second) + 1e-08) + 0.1 * master[...])

    for j in range(BLOCKS):
        for q in range(2):
            gain_grad[pl.ds(4 * j + 2 * core + q, 1), :] = gsum[2 * j + q : 2 * j + q + 1, :]
    arrive(gain_c)
    for j in range(BLOCKS):
        for q in range(2):
            gain_grad[pl.ds(4 * j + 2 * (1 - core) + q, 1), :] = gsib[2 * j + q : 2 * j + q + 1, :]

    for made in (
        ag0_a, ag1_b, ag0_b, ag1_x, ag1_a, ag0_x, rs0_x, rs1_a, rs0_b, rs1_x, rs0_a, rs1_b,
        gain_a, gain_b, gain_x, gain_c,
    ):
        for copy in made:
            copy.wait_send()
    kv_swap.wait_send()

    @pl.loop(0, BLOCKS)
    def _(j):
        swap_copy(j).wait_send()
        out_copy(j).wait()
        out_swap(j).wait_send()
        out_swap(j).wait_recv()


def on_device(normed, norm_gain, kv_cot, master, moment1, moment2):
    width = normed.shape[1]
    vmem = pl.BlockSpec(memory_space=pltpu.VMEM)
    hbm = pl.BlockSpec(memory_space=pl.ANY)
    owned = jax.ShapeDtypeStruct(master.shape, F32)
    dma = pltpu.SemaphoreType.DMA
    out = pl.pallas_call(
        kernel,
        name="zero_backward",
        out_shape=(
            owned,
            owned,
            owned,
            jax.ShapeDtypeStruct((width // 128, 128), F32),
            jax.ShapeDtypeStruct(normed.shape, BF16),
        ),
        in_specs=[hbm, vmem, hbm, vmem, vmem, vmem],
        out_specs=(vmem, vmem, vmem, vmem, hbm),
        scratch_shapes=[
            pltpu.VMEM((BLOCKS, 256, 256), BF16),
            pltpu.VMEM((256, 256), BF16),
            pltpu.VMEM((2, 2, 8, 8, 2, 16, 128), BF16),
            pltpu.VMEM((2, 2, 8, 8, 2, 16, 128), BF16),
            pltpu.VMEM((3, 8, 8, 16, 128), BF16),
            pltpu.VMEM((8, 8, 16, 128), BF16),
            pltpu.VMEM((7, 8, 16, 128), BF16),
            pltpu.VMEM((8, 16, 128), BF16),
            pltpu.VMEM((7, 16, 128), BF16),
            pltpu.VMEM((7, 2, 8, 2, 16, 128), BF16),
            pltpu.VMEM((2, 8, 2, 16, 128), BF16),
            pltpu.VMEM((3, 8, 16, 128), BF16),
            pltpu.VMEM((8, 16, 128), BF16),
            pltpu.VMEM((7, 16, 128), BF16),
            pltpu.VMEM((8, 32, 128), F32),
            pltpu.VMEM((8, 32, 128), F32),
            pltpu.VMEM((4, 32, 128), F32),
            pltpu.VMEM((32, 128), F32),
            pltpu.VMEM((32, 128), F32),
            pltpu.VMEM((BLOCKS, 256, 256), BF16),
            dma((STAGES, 7)),
            dma((STAGES, 7)),
            dma((BLOCKS + 1,)),
            dma((BLOCKS + 1,)),
            dma((BLOCKS + 1,)),
            dma((BLOCKS,)),
            dma((BLOCKS,)),
            dma((BLOCKS,)),
        ],
        compiler_params=pltpu.CompilerParams(
            collective_id=0, has_side_effects=True, vmem_limit_bytes=48 * 1024 * 1024
        ),
        cost_estimate=pl.CostEstimate(flops=1 << 30, bytes_accessed=4 << 20, transcendentals=4096),
    )(normed, norm_gain.reshape(width // 128, 128), kv_cot, master, moment1, moment2)
    return out[0], out[1], out[2], out[3].reshape(width), out[4]


def solution(mesh):
    split = P(("row", "col"), None)
    return jax.shard_map(
        on_device,
        mesh=mesh,
        in_specs=(split, P(), split, split, split, split),
        out_specs=(split, split, split, P(), split),
        check_vma=False,
    )
```

```python
import jax
import jax.numpy as jnp
from jax import lax
from jax.experimental import pallas as pl
from jax.experimental.pallas import tpu as pltpu
from jax.sharding import PartitionSpec as P

STEP = 100
TOTAL_TOKENS = 65536
SCALE = 1.0 / float(TOTAL_TOKENS) ** 0.5
MESH = pl.DeviceIdType.MESH
F32 = jnp.float32
BF16 = jnp.bfloat16

(
    AG0_A, AG1_B, AG0_B, AG1_X, AG0_X, AG1_A, AG1_P, AG1_M, AG0_P, AG0_M,
    RS0_X, RS0_XON, RS1_A, RS1_AON, RS0_B, RS1_X, RS0_A, RS1_B,
    GAIN_A, GAIN_B, GAIN_X,
) = range(21)
STAGES = 21
BLOCKS = 16
CHUNKS = 8
LOADS = 8


def kernel(
    normed, gain_hbm, kv, master_hbm,
    grad_sum, gain_sum, normed_grad,
    gain, master,
    own, sib, kv2, w, g, qx, fx, s0, rb0, t0, ra0, qf, qh, fa, s1b, rx1, t1, rb1,
    ga, gb, gx, summed0, summed1, stage, inbox,
    small, ssem, rsem, ex_send, ex_recv, ex_local, out_send, out_recv, out_local,
):
    r = lax.axis_index("row")
    c = lax.axis_index("col")
    core = lax.rem(r, 2)
    z = lax.rem(lax.div(r, 2), 8)
    xh = lax.div(r, 16)
    xl = lax.rem(c, 2)
    y = lax.div(c, 2)
    x = xh * 2 + xl
    a = z * (1 - core) + y * core
    b = y * (1 - core) + z * core

    def dev(xx, aa, bb, cc=None):
        zz = aa * (1 - core) + bb * core
        yy = bb * (1 - core) + aa * core
        cc = core if cc is None else cc
        return {"row": lax.div(xx, 2) * 16 + zz * 2 + cc, "col": yy * 2 + lax.rem(xx, 2)}

    sibling = dev(x, a, b, 1 - core)
    x_peer = [lax.rem(x + k, 4) for k in range(1, 4)]
    a_peer = [lax.rem(a + k, 8) for k in range(1, 8)]
    b_peer = [lax.rem(b + k, 8) for k in range(1, 8)]
    x_dev = [dev(v, a, b) for v in x_peer]
    a_dev = [dev(x, v, b) for v in a_peer]
    b_dev = [dev(x, a, v) for v in b_peer]

    def cols(j, cc):
        return pl.ds(pl.multiple_of(j * 512 + cc * 256, 256), 256)

    def remote(src, dst, send, recv, device):
        return pltpu.make_async_remote_copy(
            src_ref=src, dst_ref=dst, send_sem=send, recv_sem=recv,
            device_id=device, device_id_type=MESH,
        )

    def load_copy(k):
        part = pl.ds(pl.multiple_of(k * 1024, 1024), 1024)
        return pltpu.make_async_copy(normed.at[:, part], own.at[:, part], ex_local.at[k])

    def swap_copy(j):
        return remote(own.at[:, cols(j, 1 - core)], sib.at[j], ex_send.at[j], ex_recv.at[j], sibling)

    kv_load = pltpu.make_async_copy(kv, kv2.at[0], ex_local.at[BLOCKS])
    kv_swap = remote(kv2.at[0], kv2.at[1], ex_send.at[BLOCKS], ex_recv.at[BLOCKS], sibling)

    barrier = pltpu.get_barrier_semaphore()
    across_dev = [dev(v, a, b, 1 - core) for v in x_peer]
    partners = [sibling] + x_dev + across_dev + a_dev + b_dev
    for device in partners:
        pl.semaphore_signal(barrier, inc=1, device_id=device, device_id_type=MESH)

    master_load = pltpu.make_async_copy(master_hbm, master, small.at[0])
    gain_load = pltpu.make_async_copy(gain_hbm, gain, small.at[1])
    master_load.start()
    kv_load.start()

    @pl.loop(0, LOADS)
    def _(k):
        load_copy(k).start()

    gain_load.start()
    master_load.wait()
    w[0, xh, a, b, xl] = master[:, :128].astype(BF16)
    w[1, xh, a, b, xl] = master[:, 128:].astype(BF16)
    pl.semaphore_wait(barrier, len(partners))

    pending = []

    def exchange(stage_no, copies):
        made = [
            remote(src, dst, ssem.at[stage_no, k], rsem.at[stage_no, k], device)
            for k, (src, dst, device) in enumerate(copies)
        ]
        for copy in made:
            copy.start()
        pending.extend(made)
        return made

    def arrive(made):
        for copy in made:
            copy.wait_recv()

    def spread(stage_no, block, devices):
        return exchange(stage_no, [(block, block, device) for device in devices])

    def total(first, others):
        value = first.astype(F32)
        for other in others:
            value = value + other.astype(F32)
        return value

    def wrap(v, k, n):
        return lax.rem(v + k + n, n)

    xp, xm, xo = wrap(x, 1, 4), wrap(x, -1, 4), wrap(x, 2, 4)
    ap1, am1, ap2, am2 = (wrap(a, k, 8) for k in (1, -1, 2, -2))
    ap3, am3, ao = (wrap(a, k, 8) for k in (3, -3, 4))
    to_xp, to_xm = dev(xp, a, b), dev(xm, a, b)
    to_ap1, to_am1, to_ap2, to_am2 = (dev(x, v, b) for v in (ap1, am1, ap2, am2))
    low, high = pl.ds(0, 4), pl.ds(4, 4)

    def w_half(v, part):
        return w.at[0, lax.div(v, 2), part, :, lax.rem(v, 2)]

    def g_half(v, part):
        return g.at[0, lax.div(v, 2), part, :, lax.rem(v, 2)]

    st = {}

    def s1():
        st["ag0_a"] = spread(AG0_A, w.at[0, xh, a, b, xl], a_dev)
        st["ag1_b"] = spread(AG1_B, w.at[1, xh, a, b, xl], b_dev)

    def swap():
        kv_load.wait()
        kv_swap.start()

        @pl.loop(0, LOADS)
        def _(k):
            load_copy(k).wait()
            for q in range(BLOCKS // LOADS):
                swap_copy(k * (BLOCKS // LOADS) + q).start()

    def s2():
        arrive(st["ag0_a"])
        st["ag0_b"] = spread(AG0_B, w.at[0, xh, :, b, xl], b_dev)
        arrive(st["ag1_b"])
        st["ag1_x"] = spread(AG1_X, w.at[1, xh, a, :, xl], x_dev)

    def gp():
        kv_swap.wait_recv()

        @pl.loop(0, BLOCKS)
        def _(j):
            swap_copy(j).wait_recv()
            tokens = jnp.concatenate([own[:, cols(j, core)], sib[j]], axis=0)
            term = lax.dot_general(
                tokens, kv2[...].reshape(256, 256), (((0,), (0,)), ((), ())), preferred_element_type=F32
            ).astype(BF16)
            bh = lax.div(j, 8)
            bz = lax.rem(j, 8)
            for i in range(8):
                ia = bz * (1 - core) + i * core
                ib = i * (1 - core) + bz * core
                piece = term[32 * i : 32 * i + 32]
                g[0, bh, ia, ib] = piece[:, :128].reshape(2, 16, 128)
                g[1, bh, ia, ib] = piece[:, 128:].reshape(2, 16, 128)

    def s3():
        arrive(st["ag1_x"])
        plane = w.at[1, :, a]
        st["ag1_a"] = spread(AG1_A, plane, [to_ap2, to_am2, to_ap1, to_am1])
        arrive(st["ag0_b"])
        st["ag0_x"] = spread(AG0_X, w.at[0, xh, :, :, xl], [to_xp, to_xm])

    def s3_on():
        from_am2, from_ap2 = st["ag1_a"][:2]
        from_am2.wait_recv()
        far = w.at[1, :, am2]
        far_half = w.at[1, 1, am2]
        st["on_p"] = exchange(AG1_P, [(far_half, far_half, to_ap2), (far, far, to_ap1)])
        from_ap2.wait_recv()
        far = w.at[1, :, ap2]
        far_half = w.at[1, 0, ap2]
        st["on_m"] = exchange(AG1_M, [(far_half, far_half, to_am2), (far, far, to_am1)])
        from_xm, from_xp = st["ag0_x"]
        from_xm.wait_recv()
        half = w_half(xm, low)
        st["on_xp"] = exchange(AG0_P, [(half, half, to_xp)])
        from_xp.wait_recv()
        half = w_half(xp, high)
        st["on_xm"] = exchange(AG0_M, [(half, half, to_xm)])

    def s3_wait():
        arrive(st["ag1_a"][2:])
        for name in ("on_p", "on_m", "on_xp", "on_xm"):
            arrive(st[name])

    def r1():
        st["r1_a"] = exchange(
            RS1_A,
            [
                (g.at[1, 0, ao], qh.at[0], to_am2),
                (g.at[1, 1, ao], qh.at[1], to_ap2),
                (g.at[1, :, am3], qf.at[0], to_am1),
                (g.at[1, :, ap3], qf.at[1], to_ap1),
                (g.at[1, :, ap1], fa.at[0], to_ap1),
                (g.at[1, :, am1], fa.at[1], to_am1),
            ],
        )
        st["r1_x"] = exchange(
            RS0_X,
            [
                (g_half(xo, low), qx.at[0], to_xp),
                (g_half(xo, high), qx.at[1], to_xm),
                (g_half(xp, high), fx.at[0, high], to_xp),
                (g_half(xm, low), fx.at[1, low], to_xm),
            ],
        )

    def r1_on():
        arrive(st["r1_a"][:4])

        @pl.loop(0, 8)
        def _(i):
            g[1, 0, am2, i] = total(g[1, 0, am2, i], [qf[0, 0, i], qh[0, i]]).astype(BF16)
            g[1, 1, am2, i] = total(g[1, 1, am2, i], [qf[0, 1, i]]).astype(BF16)
            g[1, 0, ap2, i] = total(g[1, 0, ap2, i], [qf[1, 0, i]]).astype(BF16)
            g[1, 1, ap2, i] = total(g[1, 1, ap2, i], [qf[1, 1, i], qh[1, i]]).astype(BF16)

        st["r1_a_on"] = exchange(
            RS1_AON, [(g.at[1, :, am2], fa.at[2], to_am2), (g.at[1, :, ap2], fa.at[3], to_ap2)]
        )
        arrive(st["r1_x"][:2])
        xph, xpl, xmh, xml = lax.div(xp, 2), lax.rem(xp, 2), lax.div(xm, 2), lax.rem(xm, 2)

        @pl.loop(0, 4)
        def _(i):
            g[0, xph, i, :, xpl] = total(g[0, xph, i, :, xpl], [qx[0, i]]).astype(BF16)
            g[0, xmh, 4 + i, :, xml] = total(g[0, xmh, 4 + i, :, xml], [qx[1, i]]).astype(BF16)

        st["r1_x_on"] = exchange(
            RS0_XON,
            [(g_half(xp, low), fx.at[0, low], to_xp), (g_half(xm, high), fx.at[1, high], to_xm)],
        )

    def out_copy(j):
        return pltpu.make_async_copy(
            stage.at[j, 0], normed_grad.at[:, cols(j, core)], out_local.at[0, j]
        )

    def out_swap(j):
        return remote(stage.at[j, 1], inbox.at[j], out_send.at[j], out_recv.at[j], sibling)

    def in_copy(j):
        return pltpu.make_async_copy(
            inbox.at[j], normed_grad.at[:, cols(j, 1 - core)], out_local.at[1, j]
        )

    def mm():
        gain_load.wait()

        @pl.loop(0, BLOCKS)
        def _(j):
            bh = lax.div(j, 8)
            bz = lax.rem(j, 8)
            pieces = []
            for i in range(8):
                ia = bz * (1 - core) + i * core
                ib = i * (1 - core) + bz * core
                pieces.append(
                    jnp.concatenate(
                        [w[0, bh, ia, ib].reshape(32, 128), w[1, bh, ia, ib].reshape(32, 128)], axis=1
                    )
                )
            block = jnp.concatenate(pieces, axis=0)
            input_grad = lax.dot_general(
                kv2[...].reshape(256, 256), block, (((1,), (1,)), ((), ())), preferred_element_type=F32
            )
            row = 4 * j + 2 * core
            factor = jnp.concatenate([gain[pl.ds(row, 1), :], gain[pl.ds(row + 1, 1), :]], axis=1)
            stage[j] = (input_grad * factor).astype(BF16).reshape(2, 128, 256)
            out_copy(j).start()
            out_swap(j).start()

    shape3 = (8, 16, 128)
    diagonal = lax.broadcasted_iota(jnp.int32, shape3, 2) == (
        lax.broadcasted_iota(jnp.int32, shape3, 0) * 16 + lax.broadcasted_iota(jnp.int32, shape3, 1)
    )

    def contract(sums, weights):
        dots = jnp.sum(sums * weights.astype(F32), axis=2, keepdims=True)
        spread_out = jnp.where(diagonal, jnp.broadcast_to(dots, shape3), 0.0)
        return jnp.sum(jnp.sum(spread_out, axis=0), axis=0, keepdims=True)

    def gain_a():
        ga[a] = jnp.zeros((32, 128), F32)
        for i in range(8):
            ga[a, pl.ds(x * 8 + i, 1), :] = contract(summed0[i], w[0, xh, i, :, xl])
        for v in range(4):
            at = pl.ds(v * 8 + a, 1)
            ga[a, at, :] = ga[a, at, :] + contract(summed1[v], w[1, v // 2, a, :, v % 2])
        st["gain_a"] = spread(GAIN_A, ga.at[a], a_dev)

    def gain_b():
        arrive(st["gain_a"])
        gb[b] = total(ga[0], [ga[k] for k in range(1, 8)])
        st["gain_b"] = spread(GAIN_B, gb.at[b], b_dev)

    def gain_x():
        arrive(st["gain_b"])
        part = gx.at[core, x]
        part[...] = total(gb[0], [gb[k] for k in range(1, 8)])
        st["gain_x"] = spread(GAIN_X, part, x_dev + across_dev + [sibling])

    def gain_end():
        arrive(st["gain_x"])
        for cc in range(2):
            gain_sum[cc] = total(gx[cc, 0], [gx[cc, k] for k in range(1, 4)])

    def r2():
        arrive(st["r1_a"][4:])
        arrive(st["r1_a_on"])

        for h in range(2):
            for q in range(2):
                value = total(g[1, h, a, :, q], [fa[k, h, :, q] for k in range(4)])
                s1b[h, :, q] = value.astype(BF16)
                summed1[2 * h + q] = value

        st["r2_x"] = exchange(
            RS1_X,
            [
                (s1b.at[lax.div(v, 2), :, lax.rem(v, 2)], rx1.at[k], x_dev[k])
                for k, v in enumerate(x_peer)
            ],
        )
        arrive(st["r1_x"][2:])
        arrive(st["r1_x_on"])

        @pl.loop(0, 8)
        def _(i):
            value = total(g[0, xh, i, :, xl], [fx[k, i] for k in range(2)])
            s0[i] = value.astype(BF16)
            summed0[i] = value

        st["r2_b"] = exchange(
            RS0_B, [(s0.at[:, v], rb0.at[k], b_dev[k]) for k, v in enumerate(b_peer)]
        )

    def r3():
        arrive(st["r2_x"])
        t1[...] = total(s1b[xh, :, xl], [rx1[k] for k in range(3)]).astype(BF16)
        st["r3_b"] = exchange(
            RS1_B, [(t1.at[v], rb1.at[k], b_dev[k]) for k, v in enumerate(b_peer)]
        )
        arrive(st["r2_b"])
        t0[...] = total(s0[:, b], [rb0[k] for k in range(7)]).astype(BF16)
        st["r3_a"] = exchange(
            RS0_A, [(t0.at[v], ra0.at[k], a_dev[k]) for k, v in enumerate(a_peer)]
        )

    def r_end():
        arrive(st["r3_b"])
        grad_sum[:, 128:] = total(t1[b], [rb1[k] for k in range(7)])
        arrive(st["r3_a"])
        grad_sum[:, :128] = total(t0[a], [ra0[k] for k in range(7)])

    def end():
        for copy in pending:
            copy.wait_send()

    def end_swap():
        kv_swap.wait_send()

        @pl.loop(0, BLOCKS)
        def _(j):
            swap_copy(j).wait_send()

    def end_mm():
        @pl.loop(0, BLOCKS)
        def _(j):
            out_swap(j).wait_recv()
            in_copy(j).start()

        @pl.loop(0, BLOCKS)
        def _(j):
            out_copy(j).wait()
            out_swap(j).wait_send()
            in_copy(j).wait()

    for step in (
        s1, swap, s2, gp, r1, r1_on, s3, r2, gain_a, gain_b, s3_on, r3, gain_x, s3_wait, mm,
        r_end, gain_end, end, end_swap, end_mm,
    ):
        step()


def finish(
    grad_hbm, gain_sum_hbm, normed_grad, gain_hbm, master_hbm, moment1_hbm, moment2_hbm,
    new_master, new_moment1, new_moment2, gain_grad, normed_grad_out,
    grad_sum, gain_sum, gain, master, moment1, moment2, wide, sem, wide_sem,
):
    rows = normed_grad.shape[0] // CHUNKS
    parts = [pl.ds(rows * k, rows) for k in range(CHUNKS)]
    wide_in = [
        pltpu.make_async_copy(normed_grad.at[part], wide.at[part], wide_sem.at[0, k])
        for k, part in enumerate(parts)
    ]
    wide_out = [
        pltpu.make_async_copy(wide.at[part], normed_grad_out.at[part], wide_sem.at[1, k])
        for k, part in enumerate(parts)
    ]
    pairs = (
        (grad_hbm, grad_sum), (gain_sum_hbm, gain_sum), (gain_hbm, gain),
        (master_hbm, master), (moment1_hbm, moment1), (moment2_hbm, moment2),
    )
    loads = [pltpu.make_async_copy(src, dst, sem.at[k]) for k, (src, dst) in enumerate(pairs)]
    for copy in loads + wide_in:
        copy.start()
    for into, out in zip(wide_in, wide_out):
        into.wait()
        out.start()
    for copy in loads:
        copy.wait()
    p = lax.axis_index("row") * 16 + lax.axis_index("col")
    own_gain = jnp.broadcast_to(gain[pl.ds(lax.div(p, 8), 1), :], (16, 128))
    lane = lax.broadcasted_iota(jnp.int32, (16, 128), 1)
    sub = lax.broadcasted_iota(jnp.int32, (16, 128), 0)
    factor = jnp.sum(
        jnp.where(lane == sub + lax.rem(p, 8) * 16, own_gain, 0.0), axis=1, keepdims=True
    )
    grad = grad_sum[...] * (factor * SCALE)
    m1 = 0.9 * moment1[...] + 0.1 * grad
    m2 = 0.95 * moment2[...] + 0.05 * grad * grad
    new_moment1[...] = m1
    new_moment2[...] = m2
    first = m1 / (1.0 - 0.9**STEP)
    second = m2 / (1.0 - 0.95**STEP)
    new_master[...] = master[...] - 0.01 * (first / (jnp.sqrt(second) + 1e-08) + 0.1 * master[...])
    lane_in = lax.broadcasted_iota(jnp.int32, (128, 128), 0)
    lane_out = lax.broadcasted_iota(jnp.int32, (128, 128), 1)
    same_row = lax.rem(lane_in, 16) == lax.rem(lane_out, 16)
    group_in, group_out = lax.div(lane_in, 16), lax.div(lane_out, 16)

    def move(values, where):
        return lax.dot_general(
            values, jnp.where(same_row & where, SCALE, 0.0), (((1,), (0,)), ((), ())),
            precision=lax.Precision.HIGHEST, preferred_element_type=F32,
        )

    first0 = gain_sum[0].reshape(2, 2, 8, 128)
    for yh in range(2):
        rows0 = jnp.zeros((16, 128), F32)
        for xl in range(2):
            where = (group_in == yh * 4 + lax.div(group_out, 2)) & (lax.rem(group_out, 2) == xl)
            rows0 = rows0 + move(first0[:, xl].reshape(16, 128), where)
        for j in range(BLOCKS):
            gain_grad[4 * j + yh : 4 * j + yh + 1, :] = rows0[j : j + 1]
    z_of = lax.broadcasted_iota(jnp.int32, (8, 128), 0)
    z_lane = lax.div(lax.broadcasted_iota(jnp.int32, (8, 128), 1), 16)
    for xh in range(2):
        for yh in range(2):
            rows1 = jnp.zeros((8, 128), F32)
            for group in range(8):
                line = xh * 16 + (group % 2) * 8 + yh * 4 + group // 2
                value = jnp.where(
                    z_of == z_lane, jnp.broadcast_to(gain_sum[1, line : line + 1, :], (8, 128)), 0.0
                )
                rows1 = rows1 + move(value, group_out == group)
            for z in range(8):
                row = 4 * (xh * 8 + z) + 2 + yh
                gain_grad[row : row + 1, :] = rows1[z : z + 1]
    for copy in wide_out:
        copy.wait()


def on_device(normed, norm_gain, kv_cot, master, moment1, moment2):
    width = normed.shape[1]
    vmem = pl.BlockSpec(memory_space=pltpu.VMEM)
    anywhere = pl.BlockSpec(memory_space=pl.ANY)
    owned = jax.ShapeDtypeStruct(master.shape, F32)
    wide = jax.ShapeDtypeStruct(normed.shape, BF16)
    gain = norm_gain.reshape(width // 128, 128)
    dma = pltpu.SemaphoreType.DMA
    grad_sum, gain_sum, normed_grad = pl.pallas_call(
        kernel,
        name="zero_backward",
        out_shape=(owned, jax.ShapeDtypeStruct((2, width // 256, 128), F32), wide),
        in_specs=[anywhere] * 4,
        out_specs=(vmem, vmem, anywhere),
        scratch_shapes=[
            pltpu.VMEM((width // 128, 128), F32),
            pltpu.VMEM(master.shape, F32),
            pltpu.VMEM(normed.shape, BF16),
            pltpu.VMEM((BLOCKS, 128, 256), BF16),
            pltpu.VMEM((2, 128, 256), BF16),
            pltpu.VMEM((2, 2, 8, 8, 2, 16, 128), BF16),
            pltpu.VMEM((2, 2, 8, 8, 2, 16, 128), BF16),
            pltpu.VMEM((2, 4, 8, 16, 128), BF16),
            pltpu.VMEM((2, 8, 8, 16, 128), BF16),
            pltpu.VMEM((8, 8, 16, 128), BF16),
            pltpu.VMEM((7, 8, 16, 128), BF16),
            pltpu.VMEM((8, 16, 128), BF16),
            pltpu.VMEM((7, 16, 128), BF16),
            pltpu.VMEM((2, 2, 8, 2, 16, 128), BF16),
            pltpu.VMEM((2, 8, 2, 16, 128), BF16),
            pltpu.VMEM((4, 2, 8, 2, 16, 128), BF16),
            pltpu.VMEM((2, 8, 2, 16, 128), BF16),
            pltpu.VMEM((3, 8, 16, 128), BF16),
            pltpu.VMEM((8, 16, 128), BF16),
            pltpu.VMEM((7, 16, 128), BF16),
            pltpu.VMEM((8, 32, 128), F32),
            pltpu.VMEM((8, 32, 128), F32),
            pltpu.VMEM((2, 4, 32, 128), F32),
            pltpu.VMEM((8, 8, 16, 128), F32),
            pltpu.VMEM((4, 8, 16, 128), F32),
            pltpu.VMEM((BLOCKS, 2, 128, 256), BF16),
            pltpu.VMEM((BLOCKS, 128, 256), BF16),
            dma((2,)),
            dma((STAGES, 7)),
            dma((STAGES, 7)),
            dma((BLOCKS + 1,)),
            dma((BLOCKS + 1,)),
            dma((BLOCKS + 1,)),
            dma((BLOCKS,)),
            dma((BLOCKS,)),
            dma((2, BLOCKS)),
        ],
        compiler_params=pltpu.CompilerParams(
            collective_id=0, has_side_effects=True, vmem_limit_bytes=64 * 1024 * 1024
        ),
        cost_estimate=pl.CostEstimate(flops=1 << 30, bytes_accessed=4 << 20, transcendentals=4096),
    )(normed, gain, kv_cot, master)
    new_master, new_moment1, new_moment2, gain_grad, normed_grad = pl.pallas_call(
        finish,
        name="adamw",
        out_shape=(owned, owned, owned, jax.ShapeDtypeStruct(gain.shape, F32), wide),
        in_specs=[anywhere] * 7,
        out_specs=(vmem, vmem, vmem, vmem, anywhere),
        scratch_shapes=[
            pltpu.VMEM(master.shape, F32),
            pltpu.VMEM((2, width // 256, 128), F32),
            pltpu.VMEM(gain.shape, F32),
            pltpu.VMEM(master.shape, F32),
            pltpu.VMEM(master.shape, F32),
            pltpu.VMEM(master.shape, F32),
            pltpu.VMEM(normed.shape, BF16),
            dma((6,)),
            dma((2, CHUNKS)),
        ],
        compiler_params=pltpu.CompilerParams(vmem_limit_bytes=64 * 1024 * 1024),
    )(grad_sum, gain_sum, normed_grad, gain, master, moment1, moment2)
    return new_master, new_moment1, new_moment2, gain_grad.reshape(width), normed_grad


def solution(mesh):
    split = P(("row", "col"), None)
    return jax.shard_map(
        on_device,
        mesh=mesh,
        in_specs=(split, P(), split, split, split, split),
        out_specs=(split, split, split, P(), split),
        check_vma=False,
    )
```

```python
import math

import jax
import jax.numpy as jnp
from jax import lax
from jax.experimental import pallas as pl
from jax.experimental.pallas import tpu as pltpu
from jax.sharding import PartitionSpec as P

STEP = 100
TOTAL_TOKENS = 65536
SCALE = 1.0 / float(TOTAL_TOKENS) ** 0.5
MESH = pl.DeviceIdType.MESH
F32 = jnp.float32
BF16 = jnp.bfloat16

GROUPS = 26
BLOCKS = 16
CHUNKS = 8
LOADS = 4


def kernel(
    normed, gain_hbm, kv, master_hbm,
    grad_sum, gain_sum, normed_grad,
    gain, master,
    own, sib, kv2, w, g, qx, fx, s0, rb0, t0, ra0, qf, qh, fa, s1b, rx1, t1, rb1,
    ga, gb, gx, summed0, summed1, stage, inbox, yard, yard32,
    small, ssem, rsem, ex_send, ex_recv, ex_local, out_send, out_recv, out_local,
):
    r = lax.axis_index("row")
    c = lax.axis_index("col")
    core = lax.rem(r, 2)
    z = lax.rem(lax.div(r, 2), 8)
    xh = lax.div(r, 16)
    xl = lax.rem(c, 2)
    y = lax.div(c, 2)
    x = xh * 2 + xl
    a = z * (1 - core) + y * core
    b = y * (1 - core) + z * core

    def dev(xx, aa, bb, cc=None):
        zz = aa * (1 - core) + bb * core
        yy = bb * (1 - core) + aa * core
        cc = core if cc is None else cc
        return {"row": lax.div(xx, 2) * 16 + zz * 2 + cc, "col": yy * 2 + lax.rem(xx, 2)}

    sibling = dev(x, a, b, 1 - core)
    x_peer = [lax.rem(x + k, 4) for k in range(1, 4)]
    a_peer = [lax.rem(a + k, 8) for k in range(1, 8)]
    b_peer = [lax.rem(b + k, 8) for k in range(1, 8)]
    x_dev = [dev(v, a, b) for v in x_peer]
    a_dev = [dev(x, v, b) for v in a_peer]
    b_dev = [dev(x, a, v) for v in b_peer]

    def cols(j, cc):
        return pl.ds(pl.multiple_of(j * 512 + cc * 256, 256), 256)

    def remote(src, dst, send, recv, device):
        return pltpu.make_async_remote_copy(
            src_ref=src, dst_ref=dst, send_sem=send, recv_sem=recv,
            device_id=device, device_id_type=MESH,
        )

    def load_copy(k):
        part = pl.ds(pl.multiple_of(k * 2048, 2048), 2048)
        return pltpu.make_async_copy(normed.at[:, part], own.at[:, part], ex_local.at[k])

    def swap_copy(k, q):
        j = 4 * k + q
        return remote(own.at[:, cols(j, 1 - core)], sib.at[j], ex_send.at[0], ex_recv.at[k], sibling)

    def swap_wait(k):
        part = sib.at[pl.ds(4 * k, 4)]
        return remote(part, part, ex_send.at[0], ex_recv.at[k], sibling)

    kv_load = pltpu.make_async_copy(kv, kv2.at[0], ex_local.at[4])
    kv_swap = remote(kv2.at[0], kv2.at[1], ex_send.at[1], ex_recv.at[4], sibling)

    barrier = pltpu.get_barrier_semaphore()
    across_dev = [dev(v, a, b, 1 - core) for v in x_peer]
    partners = [sibling] + x_dev + across_dev + a_dev + b_dev
    for device in partners:
        pl.semaphore_signal(barrier, inc=1, device_id=device, device_id_type=MESH)

    master_load = pltpu.make_async_copy(master_hbm, master, small.at[0])
    gain_load = pltpu.make_async_copy(gain_hbm, gain, small.at[1])
    master_load.start()
    kv_load.start()

    @pl.loop(0, LOADS)
    def _(k):
        load_copy(k).start()

    gain_load.start()
    master_load.wait()
    w[0, xh, a, b, xl] = master[:, :128].astype(BF16)
    w[1, xh, a, b, xl] = master[:, 128:].astype(BF16)
    pl.semaphore_wait(barrier, len(partners))

    pending = []

    def group_wait(entry):
        number, tiles, dtype = entry
        counted = (yard if dtype == BF16 else yard32).at[pl.ds(0, tiles)]
        return remote(counted, counted, ssem.at[number], rsem.at[number], sibling)

    def exchange(copies):
        number = len(pending)
        tiles = 0
        for src, dst, device in copies:
            remote(src, dst, ssem.at[number], rsem.at[number], device).start()
            tiles += math.prod(src.shape) // (16 * 128)
        pending.append((number, tiles, src.dtype))
        return pending[-1]

    def arrive(entry):
        group_wait(entry).wait_recv()

    def spread(block, devices):
        return exchange([(block, block, device) for device in devices])

    def total(first, others):
        value = first.astype(F32)
        for other in others:
            value = value + other.astype(F32)
        return value

    def wrap(v, k, n):
        return lax.rem(v + k + n, n)

    xp, xm, xo = wrap(x, 1, 4), wrap(x, -1, 4), wrap(x, 2, 4)
    ap1, am1, ap2, am2 = (wrap(a, k, 8) for k in (1, -1, 2, -2))
    ap3, am3, ao = (wrap(a, k, 8) for k in (3, -3, 4))
    to_xp, to_xm = dev(xp, a, b), dev(xm, a, b)
    to_ap1, to_am1, to_ap2, to_am2 = (dev(x, v, b) for v in (ap1, am1, ap2, am2))
    low, high = pl.ds(0, 4), pl.ds(4, 4)

    def w_half(v, part):
        return w.at[0, lax.div(v, 2), part, :, lax.rem(v, 2)]

    def g_half(v, part):
        return g.at[0, lax.div(v, 2), part, :, lax.rem(v, 2)]

    st = {}

    def s1():
        st["ag0_a"] = spread(w.at[0, xh, a, b, xl], a_dev)
        st["ag1_b"] = spread(w.at[1, xh, a, b, xl], b_dev)

    def swap():
        kv_load.wait()
        kv_swap.start()

        @pl.loop(0, LOADS)
        def _(k):
            load_copy(k).wait()
            for q in range(4):
                swap_copy(k, q).start()

    def s2():
        arrive(st["ag0_a"])
        st["ag0_b"] = spread(w.at[0, xh, :, b, xl], b_dev)
        arrive(st["ag1_b"])
        st["ag1_x"] = spread(w.at[1, xh, a, :, xl], x_dev)

    def gp():
        kv_swap.wait_recv()

        @pl.loop(0, LOADS)
        def _(k):
            swap_wait(k).wait_recv()

            @pl.loop(0, 4)
            def _(q):
                j = 4 * k + q
                tokens = jnp.concatenate([own[:, cols(j, core)], sib[j]], axis=0)
                term = lax.dot_general(
                    tokens, kv2[...].reshape(256, 256), (((0,), (0,)), ((), ())),
                    preferred_element_type=F32,
                ).astype(BF16)
                bh = lax.div(j, 8)
                bz = lax.rem(j, 8)
                for i in range(8):
                    ia = bz * (1 - core) + i * core
                    ib = i * (1 - core) + bz * core
                    piece = term[32 * i : 32 * i + 32]
                    g[0, bh, ia, ib] = piece[:, :128].reshape(2, 16, 128)
                    g[1, bh, ia, ib] = piece[:, 128:].reshape(2, 16, 128)

    def s3():
        arrive(st["ag1_x"])
        plane = w.at[1, :, a]
        st["from_am2"] = spread(plane, [to_ap2])
        st["from_ap2"] = spread(plane, [to_am2])
        st["ag1_a"] = spread(plane, [to_ap1, to_am1])
        arrive(st["ag0_b"])
        st["from_xm"] = spread(w.at[0, xh, :, :, xl], [to_xp])
        st["from_xp"] = spread(w.at[0, xh, :, :, xl], [to_xm])

    def s3_on():
        arrive(st["from_am2"])
        far = w.at[1, :, am2]
        far_half = w.at[1, 1, am2]
        st["on_p"] = exchange([(far_half, far_half, to_ap2), (far, far, to_ap1)])
        arrive(st["from_ap2"])
        far = w.at[1, :, ap2]
        far_half = w.at[1, 0, ap2]
        st["on_m"] = exchange([(far_half, far_half, to_am2), (far, far, to_am1)])
        arrive(st["from_xm"])
        half = w_half(xm, low)
        st["on_xp"] = exchange([(half, half, to_xp)])
        arrive(st["from_xp"])
        half = w_half(xp, high)
        st["on_xm"] = exchange([(half, half, to_xm)])

    def s3_wait():
        arrive(st["ag1_a"])
        for name in ("on_p", "on_m", "on_xp", "on_xm"):
            arrive(st[name])

    def r1():
        st["r1_a"] = exchange([
                (g.at[1, 0, ao], qh.at[0], to_am2),
                (g.at[1, 1, ao], qh.at[1], to_ap2),
                (g.at[1, :, am3], qf.at[0], to_am1),
                (g.at[1, :, ap3], qf.at[1], to_ap1),
            ]
        )
        st["r1_a_near"] = exchange(
            [
                (g.at[1, :, ap1], fa.at[0], to_ap1),
                (g.at[1, :, am1], fa.at[1], to_am1),
            ],
        )
        st["r1_x"] = exchange([
                (g_half(xo, low), qx.at[0], to_xp),
                (g_half(xo, high), qx.at[1], to_xm),
            ]
        )
        st["r1_x_near"] = exchange(
            [
                (g_half(xp, high), fx.at[0, high], to_xp),
                (g_half(xm, low), fx.at[1, low], to_xm),
            ],
        )

    def r1_on():
        arrive(st["r1_a"])

        @pl.loop(0, 8)
        def _(i):
            g[1, 0, am2, i] = total(g[1, 0, am2, i], [qf[0, 0, i], qh[0, i]]).astype(BF16)
            g[1, 1, am2, i] = total(g[1, 1, am2, i], [qf[0, 1, i]]).astype(BF16)
            g[1, 0, ap2, i] = total(g[1, 0, ap2, i], [qf[1, 0, i]]).astype(BF16)
            g[1, 1, ap2, i] = total(g[1, 1, ap2, i], [qf[1, 1, i], qh[1, i]]).astype(BF16)

        st["r1_a_on"] = exchange([(g.at[1, :, am2], fa.at[2], to_am2), (g.at[1, :, ap2], fa.at[3], to_ap2)]
        )
        arrive(st["r1_x"])
        xph, xpl, xmh, xml = lax.div(xp, 2), lax.rem(xp, 2), lax.div(xm, 2), lax.rem(xm, 2)

        @pl.loop(0, 4)
        def _(i):
            g[0, xph, i, :, xpl] = total(g[0, xph, i, :, xpl], [qx[0, i]]).astype(BF16)
            g[0, xmh, 4 + i, :, xml] = total(g[0, xmh, 4 + i, :, xml], [qx[1, i]]).astype(BF16)

        st["r1_x_on"] = exchange([(g_half(xp, low), fx.at[0, low], to_xp), (g_half(xm, high), fx.at[1, high], to_xm)],
        )

    def out_copy(j):
        return pltpu.make_async_copy(
            stage.at[j, 0], normed_grad.at[:, cols(j, core)], out_local.at[0]
        )

    def out_swap(j):
        return remote(stage.at[j, 1], inbox.at[j], out_send, out_recv.at[lax.div(j, 4)], sibling)

    def in_copy(j):
        return pltpu.make_async_copy(
            inbox.at[j], normed_grad.at[:, cols(j, 1 - core)], out_local.at[1]
        )

    def mm():
        gain_load.wait()

        @pl.loop(0, BLOCKS)
        def _(j):
            bh = lax.div(j, 8)
            bz = lax.rem(j, 8)
            pieces = []
            for i in range(8):
                ia = bz * (1 - core) + i * core
                ib = i * (1 - core) + bz * core
                pieces.append(
                    jnp.concatenate(
                        [w[0, bh, ia, ib].reshape(32, 128), w[1, bh, ia, ib].reshape(32, 128)], axis=1
                    )
                )
            block = jnp.concatenate(pieces, axis=0)
            input_grad = lax.dot_general(
                kv2[...].reshape(256, 256), block, (((1,), (1,)), ((), ())), preferred_element_type=F32
            )
            row = 4 * j + 2 * core
            factor = jnp.concatenate([gain[pl.ds(row, 1), :], gain[pl.ds(row + 1, 1), :]], axis=1)
            stage[j] = (input_grad * factor).astype(BF16).reshape(2, 128, 256)
            out_copy(j).start()
            out_swap(j).start()

    shape3 = (8, 16, 128)
    diagonal = lax.broadcasted_iota(jnp.int32, shape3, 2) == (
        lax.broadcasted_iota(jnp.int32, shape3, 0) * 16 + lax.broadcasted_iota(jnp.int32, shape3, 1)
    )

    def contract(sums, weights):
        dots = jnp.sum(sums * weights.astype(F32), axis=2, keepdims=True)
        spread_out = jnp.where(diagonal, jnp.broadcast_to(dots, shape3), 0.0)
        return jnp.sum(jnp.sum(spread_out, axis=0), axis=0, keepdims=True)

    def gain_a():
        ga[a] = jnp.zeros((32, 128), F32)
        for i in range(8):
            ga[a, pl.ds(x * 8 + i, 1), :] = contract(summed0[i], w[0, xh, i, :, xl])
        for v in range(4):
            at = pl.ds(v * 8 + a, 1)
            ga[a, at, :] = ga[a, at, :] + contract(summed1[v], w[1, v // 2, a, :, v % 2])
        st["gain_a"] = spread(ga.at[a], a_dev)

    def gain_b():
        arrive(st["gain_a"])
        gb[b] = total(ga[0], [ga[k] for k in range(1, 8)])
        st["gain_b"] = spread(gb.at[b], b_dev)

    def gain_x():
        arrive(st["gain_b"])
        part = gx.at[core, x]
        part[...] = total(gb[0], [gb[k] for k in range(1, 8)])
        st["gain_x"] = spread(part, x_dev + across_dev + [sibling])

    def gain_end():
        arrive(st["gain_x"])
        for cc in range(2):
            gain_sum[cc] = total(gx[cc, 0], [gx[cc, k] for k in range(1, 4)])

    def r2():
        arrive(st["r1_a_near"])
        arrive(st["r1_a_on"])

        for h in range(2):
            for q in range(2):
                value = total(g[1, h, a, :, q], [fa[k, h, :, q] for k in range(4)])
                s1b[h, :, q] = value.astype(BF16)
                summed1[2 * h + q] = value

        st["r2_x"] = exchange([
                (s1b.at[lax.div(v, 2), :, lax.rem(v, 2)], rx1.at[k], x_dev[k])
                for k, v in enumerate(x_peer)
            ],
        )
        arrive(st["r1_x_near"])
        arrive(st["r1_x_on"])

        @pl.loop(0, 8)
        def _(i):
            value = total(g[0, xh, i, :, xl], [fx[k, i] for k in range(2)])
            s0[i] = value.astype(BF16)
            summed0[i] = value

        st["r2_b"] = exchange([(s0.at[:, v], rb0.at[k], b_dev[k]) for k, v in enumerate(b_peer)]
        )

    def r3():
        arrive(st["r2_x"])
        t1[...] = total(s1b[xh, :, xl], [rx1[k] for k in range(3)]).astype(BF16)
        st["r3_b"] = exchange([(t1.at[v], rb1.at[k], b_dev[k]) for k, v in enumerate(b_peer)]
        )
        arrive(st["r2_b"])
        t0[...] = total(s0[:, b], [rb0[k] for k in range(7)]).astype(BF16)
        st["r3_a"] = exchange([(t0.at[v], ra0.at[k], a_dev[k]) for k, v in enumerate(a_peer)]
        )

    def r_end():
        arrive(st["r3_b"])
        grad_sum[:, 128:] = total(t1[b], [rb1[k] for k in range(7)])
        arrive(st["r3_a"])
        grad_sum[:, :128] = total(t0[a], [ra0[k] for k in range(7)])

    def end():
        for entry in pending:
            group_wait(entry).wait_send()

    def end_swap():
        kv_swap.wait_send()
        remote(sib, sib, ex_send.at[0], ex_recv.at[0], sibling).wait_send()

    def end_mm():
        for k in range(4):
            part = inbox.at[pl.ds(4 * k, 4)]
            remote(part, part, out_send, out_recv.at[k], sibling).wait_recv()
            for q in range(4):
                in_copy(4 * k + q).start()
        remote(inbox, inbox, out_send, out_recv.at[0], sibling).wait_send()
        for k in range(2):
            pltpu.make_async_copy(inbox, inbox, out_local.at[k]).wait()

    for step in (
        s1, swap, s2, gp, r1, r1_on, s3, r2, gain_a, gain_b, s3_on, r3, gain_x, s3_wait, mm,
        r_end, gain_end, end, end_swap, end_mm,
    ):
        step()


def finish(
    grad_hbm, gain_sum_hbm, normed_grad, gain_hbm, master_hbm, moment1_hbm, moment2_hbm,
    new_master, new_moment1, new_moment2, gain_grad, normed_grad_out,
    grad_sum, gain_sum, gain, master, moment1, moment2, wide, sem, wide_sem,
):
    rows = normed_grad.shape[0] // CHUNKS
    parts = [pl.ds(rows * k, rows) for k in range(CHUNKS)]
    wide_in = [
        pltpu.make_async_copy(normed_grad.at[part], wide.at[part], wide_sem.at[0, k])
        for k, part in enumerate(parts)
    ]
    wide_out = [
        pltpu.make_async_copy(wide.at[part], normed_grad_out.at[part], wide_sem.at[1, k])
        for k, part in enumerate(parts)
    ]
    pairs = (
        (grad_hbm, grad_sum), (gain_sum_hbm, gain_sum), (gain_hbm, gain),
        (master_hbm, master), (moment1_hbm, moment1), (moment2_hbm, moment2),
    )
    loads = [pltpu.make_async_copy(src, dst, sem.at[k]) for k, (src, dst) in enumerate(pairs)]
    for copy in loads + wide_in:
        copy.start()
    def pass_on(first, last):
        for into, out in zip(wide_in[first:last], wide_out[first:last]):
            into.wait()
            out.start()

    for copy in loads:
        copy.wait()
    p = lax.axis_index("row") * 16 + lax.axis_index("col")
    own_gain = jnp.broadcast_to(gain[pl.ds(lax.div(p, 8), 1), :], (16, 128))
    lane = lax.broadcasted_iota(jnp.int32, (16, 128), 1)
    sub = lax.broadcasted_iota(jnp.int32, (16, 128), 0)
    factor = jnp.sum(
        jnp.where(lane == sub + lax.rem(p, 8) * 16, own_gain, 0.0), axis=1, keepdims=True
    )
    grad = grad_sum[...] * (factor * SCALE)
    m1 = 0.9 * moment1[...] + 0.1 * grad
    m2 = 0.95 * moment2[...] + 0.05 * grad * grad
    new_moment1[...] = m1
    new_moment2[...] = m2
    first = m1 / (1.0 - 0.9**STEP)
    second = m2 / (1.0 - 0.95**STEP)
    new_master[...] = master[...] - 0.01 * (first / (jnp.sqrt(second) + 1e-08) + 0.1 * master[...])
    pass_on(0, CHUNKS)
    lane_in = lax.broadcasted_iota(jnp.int32, (128, 128), 0)
    lane_out = lax.broadcasted_iota(jnp.int32, (128, 128), 1)
    same_row = lax.rem(lane_in, 16) == lax.rem(lane_out, 16)
    group_in, group_out = lax.div(lane_in, 16), lax.div(lane_out, 16)

    def move(values, where):
        high = values.astype(BF16)
        rest = values - high.astype(F32)
        middle = rest.astype(BF16)
        low = (rest - middle.astype(F32)).astype(BF16)
        places = jnp.where(same_row & where, SCALE, 0.0).astype(BF16)
        moved = lax.dot_general(
            jnp.concatenate([high, middle, low], axis=0), places, (((1,), (0,)), ((), ())),
            preferred_element_type=F32,
        )
        count = values.shape[0]
        return moved[:count] + (moved[count : 2 * count] + moved[2 * count :])

    first0 = gain_sum[0].reshape(2, 2, 8, 128)
    for yh in range(2):
        rows0 = jnp.zeros((16, 128), F32)
        for xl in range(2):
            where = (group_in == yh * 4 + lax.div(group_out, 2)) & (lax.rem(group_out, 2) == xl)
            rows0 = rows0 + move(first0[:, xl].reshape(16, 128), where)
        for j in range(BLOCKS):
            gain_grad[4 * j + yh : 4 * j + yh + 1, :] = rows0[j : j + 1]
    z_of = lax.broadcasted_iota(jnp.int32, (8, 128), 0)
    z_lane = lax.div(lax.broadcasted_iota(jnp.int32, (8, 128), 1), 16)
    rows1 = jnp.zeros((32, 128), F32)
    for group in range(8):
        values = []
        for quarter in range(4):
            line = (quarter // 2) * 16 + (group % 2) * 8 + (quarter % 2) * 4 + group // 2
            one = jnp.broadcast_to(gain_sum[1, line : line + 1, :], (8, 128))
            values.append(jnp.where(z_of == z_lane, one, 0.0))
        rows1 = rows1 + move(jnp.concatenate(values, axis=0), group_out == group)
    for quarter in range(4):
        for z in range(8):
            row = 4 * ((quarter // 2) * 8 + z) + 2 + quarter % 2
            gain_grad[row : row + 1, :] = rows1[quarter * 8 + z : quarter * 8 + z + 1]
    for copy in wide_out:
        copy.wait()


def on_device(normed, norm_gain, kv_cot, master, moment1, moment2):
    width = normed.shape[1]
    vmem = pl.BlockSpec(memory_space=pltpu.VMEM)
    anywhere = pl.BlockSpec(memory_space=pl.ANY)
    owned = jax.ShapeDtypeStruct(master.shape, F32)
    wide = jax.ShapeDtypeStruct(normed.shape, BF16)
    gain = norm_gain.reshape(width // 128, 128)
    dma = pltpu.SemaphoreType.DMA
    grad_sum, gain_sum, normed_grad = pl.pallas_call(
        kernel,
        name="zero_backward",
        out_shape=(owned, jax.ShapeDtypeStruct((2, width // 256, 128), F32), wide),
        in_specs=[anywhere] * 4,
        out_specs=(vmem, vmem, anywhere),
        scratch_shapes=[
            pltpu.VMEM((width // 128, 128), F32),
            pltpu.VMEM(master.shape, F32),
            pltpu.VMEM(normed.shape, BF16),
            pltpu.VMEM((BLOCKS, 128, 256), BF16),
            pltpu.VMEM((2, 128, 256), BF16),
            pltpu.VMEM((2, 2, 8, 8, 2, 16, 128), BF16),
            pltpu.VMEM((2, 2, 8, 8, 2, 16, 128), BF16),
            pltpu.VMEM((2, 4, 8, 16, 128), BF16),
            pltpu.VMEM((2, 8, 8, 16, 128), BF16),
            pltpu.VMEM((8, 8, 16, 128), BF16),
            pltpu.VMEM((7, 8, 16, 128), BF16),
            pltpu.VMEM((8, 16, 128), BF16),
            pltpu.VMEM((7, 16, 128), BF16),
            pltpu.VMEM((2, 2, 8, 2, 16, 128), BF16),
            pltpu.VMEM((2, 8, 2, 16, 128), BF16),
            pltpu.VMEM((4, 2, 8, 2, 16, 128), BF16),
            pltpu.VMEM((2, 8, 2, 16, 128), BF16),
            pltpu.VMEM((3, 8, 16, 128), BF16),
            pltpu.VMEM((8, 16, 128), BF16),
            pltpu.VMEM((7, 16, 128), BF16),
            pltpu.VMEM((8, 32, 128), F32),
            pltpu.VMEM((8, 32, 128), F32),
            pltpu.VMEM((2, 4, 32, 128), F32),
            pltpu.VMEM((8, 8, 16, 128), F32),
            pltpu.VMEM((4, 8, 16, 128), F32),
            pltpu.VMEM((BLOCKS, 2, 128, 256), BF16),
            pltpu.VMEM((BLOCKS, 128, 256), BF16),
            pltpu.VMEM((128, 16, 128), BF16),
            pltpu.VMEM((16, 16, 128), F32),
            dma((2,)),
            dma((GROUPS,)),
            dma((GROUPS,)),
            dma((2,)),
            dma((LOADS + 1,)),
            dma((LOADS + 1,)),
            dma,
            dma((4,)),
            dma((2,)),
        ],
        compiler_params=pltpu.CompilerParams(
            collective_id=0, has_side_effects=True, vmem_limit_bytes=64 * 1024 * 1024
        ),
        cost_estimate=pl.CostEstimate(flops=1 << 30, bytes_accessed=4 << 20, transcendentals=4096),
    )(normed, gain, kv_cot, master)
    new_master, new_moment1, new_moment2, gain_grad, normed_grad = pl.pallas_call(
        finish,
        name="adamw",
        out_shape=(owned, owned, owned, jax.ShapeDtypeStruct(gain.shape, F32), wide),
        in_specs=[anywhere] * 7,
        out_specs=(vmem, vmem, vmem, vmem, anywhere),
        scratch_shapes=[
            pltpu.VMEM(master.shape, F32),
            pltpu.VMEM((2, width // 256, 128), F32),
            pltpu.VMEM(gain.shape, F32),
            pltpu.VMEM(master.shape, F32),
            pltpu.VMEM(master.shape, F32),
            pltpu.VMEM(master.shape, F32),
            pltpu.VMEM(normed.shape, BF16),
            dma((6,)),
            dma((2, CHUNKS)),
        ],
        compiler_params=pltpu.CompilerParams(vmem_limit_bytes=64 * 1024 * 1024),
    )(grad_sum, gain_sum, normed_grad, gain, master, moment1, moment2)
    return new_master, new_moment1, new_moment2, gain_grad.reshape(width), normed_grad


def solution(mesh):
    split = P(("row", "col"), None)
    return jax.shard_map(
        on_device,
        mesh=mesh,
        in_specs=(split, P(), split, split, split, split),
        out_specs=(split, split, split, P(), split),
        check_vma=False,
    )
```

```python
import math

import jax
import jax.numpy as jnp
from jax import lax
from jax.experimental import pallas as pl
from jax.experimental.pallas import tpu as pltpu
from jax.sharding import PartitionSpec as P

STEP = 100
TOTAL_TOKENS = 65536
SCALE = 1.0 / float(TOTAL_TOKENS) ** 0.5
MESH = pl.DeviceIdType.MESH
F32 = jnp.float32
BF16 = jnp.bfloat16

GROUPS = 26
BLOCKS = 16
CHUNKS = 8
LOADS = 4


def kernel(
    normed, gain_hbm, kv, master_hbm,
    grad_sum, gain_sum, normed_grad,
    gain, master,
    own, sib, kv2, w, g, qx, fx, s0, rb0, t0, ra0, qf, qh, fa, s1b, rx1, t1, rb1,
    ga, gb, gx, summed0, summed1, stage, inbox, yard, yard32,
    small, ssem, rsem, ex_send, ex_recv, ex_local, out_send, out_recv, out_local,
):
    r = lax.axis_index("row")
    c = lax.axis_index("col")
    core = lax.rem(r, 2)
    z = lax.rem(lax.div(r, 2), 8)
    xh = lax.div(r, 16)
    xl = lax.rem(c, 2)
    y = lax.div(c, 2)
    x = xh * 2 + xl
    a = z * (1 - core) + y * core
    b = y * (1 - core) + z * core

    def dev(xx, aa, bb, cc=None):
        zz = aa * (1 - core) + bb * core
        yy = bb * (1 - core) + aa * core
        cc = core if cc is None else cc
        return {"row": lax.div(xx, 2) * 16 + zz * 2 + cc, "col": yy * 2 + lax.rem(xx, 2)}

    sibling = dev(x, a, b, 1 - core)
    x_peer = [lax.rem(x + k, 4) for k in range(1, 4)]
    a_peer = [lax.rem(a + k, 8) for k in range(1, 8)]
    b_peer = [lax.rem(b + k, 8) for k in range(1, 8)]
    x_dev = [dev(v, a, b) for v in x_peer]
    a_dev = [dev(x, v, b) for v in a_peer]
    b_dev = [dev(x, a, v) for v in b_peer]

    def cols(j, cc):
        return pl.ds(pl.multiple_of(j * 512 + cc * 256, 256), 256)

    def remote(src, dst, send, recv, device):
        return pltpu.make_async_remote_copy(
            src_ref=src, dst_ref=dst, send_sem=send, recv_sem=recv,
            device_id=device, device_id_type=MESH,
        )

    def load_copy(k):
        part = pl.ds(pl.multiple_of(k * 2048, 2048), 2048)
        return pltpu.make_async_copy(normed.at[:, part], own.at[:, part], ex_local.at[k])

    def swap_copy(k, q):
        j = 4 * k + q
        return remote(own.at[:, cols(j, 1 - core)], sib.at[j], ex_send.at[0], ex_recv.at[k], sibling)

    def swap_wait(k):
        part = sib.at[pl.ds(4 * k, 4)]
        return remote(part, part, ex_send.at[0], ex_recv.at[k], sibling)

    kv_load = pltpu.make_async_copy(kv, kv2.at[0], ex_local.at[4])
    kv_swap = remote(kv2.at[0], kv2.at[1], ex_send.at[1], ex_recv.at[4], sibling)

    barrier = pltpu.get_barrier_semaphore()
    across_dev = [dev(v, a, b, 1 - core) for v in x_peer]
    partners = [sibling] + x_dev + across_dev + a_dev + b_dev
    for device in partners:
        pl.semaphore_signal(barrier, inc=1, device_id=device, device_id_type=MESH)

    master_load = pltpu.make_async_copy(master_hbm, master, small.at[0])
    gain_load = pltpu.make_async_copy(gain_hbm, gain, small.at[1])
    master_load.start()
    kv_load.start()

    @pl.loop(0, LOADS)
    def _(k):
        load_copy(k).start()

    gain_load.start()
    master_load.wait()
    w[0, xh, a, b, xl] = master[:, :128].astype(BF16)
    w[1, xh, a, b, xl] = master[:, 128:].astype(BF16)
    pl.semaphore_wait(barrier, len(partners))

    pending = []

    def group_wait(entry):
        number, tiles, dtype = entry
        counted = (yard if dtype == BF16 else yard32).at[pl.ds(0, tiles)]
        return remote(counted, counted, ssem.at[number], rsem.at[number], sibling)

    def exchange(copies):
        number = len(pending)
        tiles = 0
        for src, dst, device in copies:
            remote(src, dst, ssem.at[number], rsem.at[number], device).start()
            tiles += math.prod(src.shape) // (16 * 128)
        pending.append((number, tiles, src.dtype))
        return pending[-1]

    def arrive(entry):
        group_wait(entry).wait_recv()

    def spread(block, devices):
        return exchange([(block, block, device) for device in devices])

    def total(first, others):
        value = first.astype(F32)
        for other in others:
            value = value + other.astype(F32)
        return value

    def wrap(v, k, n):
        return lax.rem(v + k + n, n)

    xp, xm, xo = wrap(x, 1, 4), wrap(x, -1, 4), wrap(x, 2, 4)
    ap1, am1, ap2, am2 = (wrap(a, k, 8) for k in (1, -1, 2, -2))
    ap3, am3, ao = (wrap(a, k, 8) for k in (3, -3, 4))
    to_xp, to_xm = dev(xp, a, b), dev(xm, a, b)
    to_ap1, to_am1, to_ap2, to_am2 = (dev(x, v, b) for v in (ap1, am1, ap2, am2))
    low, high = pl.ds(0, 4), pl.ds(4, 4)

    def w_half(v, part):
        return w.at[0, lax.div(v, 2), part, :, lax.rem(v, 2)]

    def g_half(v, part):
        return g.at[0, lax.div(v, 2), part, :, lax.rem(v, 2)]

    st = {}

    def s1():
        st["ag0_a"] = spread(w.at[0, xh, a, b, xl], a_dev)
        st["ag1_b"] = spread(w.at[1, xh, a, b, xl], b_dev)

    def swap():
        kv_load.wait()
        kv_swap.start()

        @pl.loop(0, LOADS)
        def _(k):
            load_copy(k).wait()
            for q in range(4):
                swap_copy(k, q).start()

    def s2():
        arrive(st["ag0_a"])
        st["ag0_b"] = spread(w.at[0, xh, :, b, xl], b_dev)
        arrive(st["ag1_b"])
        st["ag1_x"] = spread(w.at[1, xh, a, :, xl], x_dev)

    def gp():
        kv_swap.wait_recv()

        @pl.loop(0, LOADS)
        def _(k):
            swap_wait(k).wait_recv()

            @pl.loop(0, 4)
            def _(q):
                j = 4 * k + q
                tokens = jnp.concatenate([own[:, cols(j, core)], sib[j]], axis=0)
                term = lax.dot_general(
                    tokens, kv2[...].reshape(256, 256), (((0,), (0,)), ((), ())),
                    preferred_element_type=F32,
                ).astype(BF16)
                bh = lax.div(j, 8)
                bz = lax.rem(j, 8)
                for i in range(8):
                    ia = bz * (1 - core) + i * core
                    ib = i * (1 - core) + bz * core
                    piece = term[32 * i : 32 * i + 32]
                    g[0, bh, ia, ib] = piece[:, :128].reshape(2, 16, 128)
                    g[1, bh, ia, ib] = piece[:, 128:].reshape(2, 16, 128)

    def s3():
        arrive(st["ag1_x"])
        plane = w.at[1, :, a]
        st["from_am2"] = spread(plane, [to_ap2])
        st["from_ap2"] = spread(plane, [to_am2])
        st["ag1_a"] = spread(plane, [to_ap1, to_am1])
        arrive(st["ag0_b"])
        st["from_xm"] = spread(w.at[0, xh, :, :, xl], [to_xp])
        st["from_xp"] = spread(w.at[0, xh, :, :, xl], [to_xm])

    def s3_on():
        arrive(st["from_am2"])
        far = w.at[1, :, am2]
        far_half = w.at[1, 1, am2]
        st["on_p"] = exchange([(far_half, far_half, to_ap2), (far, far, to_ap1)])
        arrive(st["from_ap2"])
        far = w.at[1, :, ap2]
        far_half = w.at[1, 0, ap2]
        st["on_m"] = exchange([(far_half, far_half, to_am2), (far, far, to_am1)])
        arrive(st["from_xm"])
        half = w_half(xm, low)
        st["on_xp"] = exchange([(half, half, to_xp)])
        arrive(st["from_xp"])
        half = w_half(xp, high)
        st["on_xm"] = exchange([(half, half, to_xm)])

    def s3_wait():
        arrive(st["ag1_a"])
        for name in ("on_p", "on_m", "on_xp", "on_xm"):
            arrive(st[name])

    def r1():
        st["r1_a"] = exchange([
                (g.at[1, 0, ao], qh.at[0], to_am2),
                (g.at[1, 1, ao], qh.at[1], to_ap2),
                (g.at[1, :, am3], qf.at[0], to_am1),
                (g.at[1, :, ap3], qf.at[1], to_ap1),
            ]
        )
        st["r1_a_near"] = exchange(
            [
                (g.at[1, :, ap1], fa.at[0], to_ap1),
                (g.at[1, :, am1], fa.at[1], to_am1),
            ],
        )
        st["r1_x"] = exchange([
                (g_half(xo, low), qx.at[0], to_xp),
                (g_half(xo, high), qx.at[1], to_xm),
            ]
        )
        st["r1_x_near"] = exchange(
            [
                (g_half(xp, high), fx.at[0, high], to_xp),
                (g_half(xm, low), fx.at[1, low], to_xm),
            ],
        )

    def r1_on():
        arrive(st["r1_a"])

        @pl.loop(0, 8)
        def _(i):
            g[1, 0, am2, i] = total(g[1, 0, am2, i], [qf[0, 0, i], qh[0, i]]).astype(BF16)
            g[1, 1, am2, i] = total(g[1, 1, am2, i], [qf[0, 1, i]]).astype(BF16)
            g[1, 0, ap2, i] = total(g[1, 0, ap2, i], [qf[1, 0, i]]).astype(BF16)
            g[1, 1, ap2, i] = total(g[1, 1, ap2, i], [qf[1, 1, i], qh[1, i]]).astype(BF16)

        st["r1_a_on"] = exchange([(g.at[1, :, am2], fa.at[2], to_am2), (g.at[1, :, ap2], fa.at[3], to_ap2)]
        )
        arrive(st["r1_x"])
        xph, xpl, xmh, xml = lax.div(xp, 2), lax.rem(xp, 2), lax.div(xm, 2), lax.rem(xm, 2)

        @pl.loop(0, 4)
        def _(i):
            g[0, xph, i, :, xpl] = total(g[0, xph, i, :, xpl], [qx[0, i]]).astype(BF16)
            g[0, xmh, 4 + i, :, xml] = total(g[0, xmh, 4 + i, :, xml], [qx[1, i]]).astype(BF16)

        st["r1_x_on"] = exchange([(g_half(xp, low), fx.at[0, low], to_xp), (g_half(xm, high), fx.at[1, high], to_xm)],
        )

    def out_copy(j):
        return pltpu.make_async_copy(
            stage.at[j, 0], normed_grad.at[:, cols(j, core)], out_local.at[0]
        )

    def out_swap(j):
        return remote(stage.at[j, 1], inbox.at[j], out_send, out_recv.at[lax.div(j, 4)], sibling)

    def in_copy(j):
        return pltpu.make_async_copy(
            inbox.at[j], normed_grad.at[:, cols(j, 1 - core)], out_local.at[1]
        )

    def mm():
        gain_load.wait()

        @pl.loop(0, BLOCKS)
        def _(j):
            bh = lax.div(j, 8)
            bz = lax.rem(j, 8)
            pieces = []
            for i in range(8):
                ia = bz * (1 - core) + i * core
                ib = i * (1 - core) + bz * core
                pieces.append(
                    jnp.concatenate(
                        [w[0, bh, ia, ib].reshape(32, 128), w[1, bh, ia, ib].reshape(32, 128)], axis=1
                    )
                )
            block = jnp.concatenate(pieces, axis=0)
            input_grad = lax.dot_general(
                kv2[...].reshape(256, 256), block, (((1,), (1,)), ((), ())), preferred_element_type=F32
            )
            row = 4 * j + 2 * core
            factor = jnp.concatenate([gain[pl.ds(row, 1), :], gain[pl.ds(row + 1, 1), :]], axis=1)
            stage[j] = (input_grad * factor).astype(BF16).reshape(2, 128, 256)
            out_copy(j).start()
            out_swap(j).start()

    shape3 = (8, 16, 128)
    diagonal = lax.broadcasted_iota(jnp.int32, shape3, 2) == (
        lax.broadcasted_iota(jnp.int32, shape3, 0) * 16 + lax.broadcasted_iota(jnp.int32, shape3, 1)
    )

    def contract(sums, weights):
        dots = jnp.sum(sums * weights.astype(F32), axis=2, keepdims=True)
        spread_out = jnp.where(diagonal, jnp.broadcast_to(dots, shape3), 0.0)
        return jnp.sum(jnp.sum(spread_out, axis=0), axis=0, keepdims=True)

    def gain_a():
        ga[a] = jnp.zeros((32, 128), F32)
        for i in range(8):
            ga[a, pl.ds(x * 8 + i, 1), :] = contract(summed0[i], w[0, xh, i, :, xl])
        for v in range(4):
            at = pl.ds(v * 8 + a, 1)
            ga[a, at, :] = ga[a, at, :] + contract(summed1[v], w[1, v // 2, a, :, v % 2])
        st["gain_a"] = spread(ga.at[a], a_dev)

    def gain_b():
        arrive(st["gain_a"])
        gb[b] = total(ga[0], [ga[k] for k in range(1, 8)])
        st["gain_b"] = spread(gb.at[b], b_dev)

    def gain_x():
        arrive(st["gain_b"])
        part = gx.at[core, x]
        part[...] = total(gb[0], [gb[k] for k in range(1, 8)])
        st["gain_x"] = spread(part, x_dev + across_dev + [sibling])

    def gain_end():
        arrive(st["gain_x"])
        for cc in range(2):
            gain_sum[cc] = total(gx[cc, 0], [gx[cc, k] for k in range(1, 4)])

    def r2():
        arrive(st["r1_a_near"])
        arrive(st["r1_a_on"])

        for h in range(2):
            for q in range(2):
                value = total(g[1, h, a, :, q], [fa[k, h, :, q] for k in range(4)])
                s1b[h, :, q] = value.astype(BF16)
                summed1[2 * h + q] = value

        st["r2_x"] = exchange([
                (s1b.at[lax.div(v, 2), :, lax.rem(v, 2)], rx1.at[k], x_dev[k])
                for k, v in enumerate(x_peer)
            ],
        )
        arrive(st["r1_x_near"])
        arrive(st["r1_x_on"])

        @pl.loop(0, 8)
        def _(i):
            value = total(g[0, xh, i, :, xl], [fx[k, i] for k in range(2)])
            s0[i] = value.astype(BF16)
            summed0[i] = value

        st["r2_b"] = exchange([(s0.at[:, v], rb0.at[k], b_dev[k]) for k, v in enumerate(b_peer)]
        )

    def r3():
        arrive(st["r2_x"])
        t1[...] = total(s1b[xh, :, xl], [rx1[k] for k in range(3)]).astype(BF16)
        st["r3_b"] = exchange([(t1.at[v], rb1.at[k], b_dev[k]) for k, v in enumerate(b_peer)]
        )
        arrive(st["r2_b"])
        t0[...] = total(s0[:, b], [rb0[k] for k in range(7)]).astype(BF16)
        st["r3_a"] = exchange([(t0.at[v], ra0.at[k], a_dev[k]) for k, v in enumerate(a_peer)]
        )

    def r_end():
        arrive(st["r3_b"])
        grad_sum[:, 128:] = total(t1[b], [rb1[k] for k in range(7)])
        arrive(st["r3_a"])
        grad_sum[:, :128] = total(t0[a], [ra0[k] for k in range(7)])

    def end():
        for entry in pending:
            group_wait(entry).wait_send()

    def end_swap():
        kv_swap.wait_send()
        remote(sib, sib, ex_send.at[0], ex_recv.at[0], sibling).wait_send()

    def end_mm():
        for k in range(4):
            part = inbox.at[pl.ds(4 * k, 4)]
            remote(part, part, out_send, out_recv.at[k], sibling).wait_recv()
            for q in range(4):
                in_copy(4 * k + q).start()
        remote(inbox, inbox, out_send, out_recv.at[0], sibling).wait_send()
        for k in range(2):
            pltpu.make_async_copy(inbox, inbox, out_local.at[k]).wait()

    for step in (
        s1, swap, gp, r1, s2, r1_on, s3, r2, gain_a, s3_on, gain_b, r3, gain_x, s3_wait, mm,
        r_end, gain_end, end, end_swap, end_mm,
    ):
        step()


def finish(
    grad_hbm, gain_sum_hbm, normed_grad, gain_hbm, master_hbm, moment1_hbm, moment2_hbm,
    new_master, new_moment1, new_moment2, gain_grad, normed_grad_out,
    grad_sum, gain_sum, gain, master, moment1, moment2, wide, sem, wide_sem,
):
    rows = normed_grad.shape[0] // CHUNKS
    parts = [pl.ds(rows * k, rows) for k in range(CHUNKS)]
    wide_in = [
        pltpu.make_async_copy(normed_grad.at[part], wide.at[part], wide_sem.at[0, k])
        for k, part in enumerate(parts)
    ]
    wide_out = [
        pltpu.make_async_copy(wide.at[part], normed_grad_out.at[part], wide_sem.at[1, k])
        for k, part in enumerate(parts)
    ]
    pairs = (
        (grad_hbm, grad_sum), (gain_sum_hbm, gain_sum), (gain_hbm, gain),
        (master_hbm, master), (moment1_hbm, moment1), (moment2_hbm, moment2),
    )
    loads = [pltpu.make_async_copy(src, dst, sem.at[k]) for k, (src, dst) in enumerate(pairs)]
    for copy in loads + wide_in:
        copy.start()
    def pass_on(first, last):
        for into, out in zip(wide_in[first:last], wide_out[first:last]):
            into.wait()
            out.start()

    for copy in loads:
        copy.wait()
    p = lax.axis_index("row") * 16 + lax.axis_index("col")
    own_gain = jnp.broadcast_to(gain[pl.ds(lax.div(p, 8), 1), :], (16, 128))
    lane = lax.broadcasted_iota(jnp.int32, (16, 128), 1)
    sub = lax.broadcasted_iota(jnp.int32, (16, 128), 0)
    factor = jnp.sum(
        jnp.where(lane == sub + lax.rem(p, 8) * 16, own_gain, 0.0), axis=1, keepdims=True
    )
    grad = grad_sum[...] * (factor * SCALE)
    m1 = 0.9 * moment1[...] + 0.1 * grad
    m2 = 0.95 * moment2[...] + 0.05 * grad * grad
    new_moment1[...] = m1
    new_moment2[...] = m2
    first = m1 / (1.0 - 0.9**STEP)
    second = m2 / (1.0 - 0.95**STEP)
    new_master[...] = master[...] - 0.01 * (first / (jnp.sqrt(second) + 1e-08) + 0.1 * master[...])
    pass_on(0, CHUNKS)
    lane_in = lax.broadcasted_iota(jnp.int32, (128, 128), 0)
    lane_out = lax.broadcasted_iota(jnp.int32, (128, 128), 1)
    same_row = lax.rem(lane_in, 16) == lax.rem(lane_out, 16)
    group_in, group_out = lax.div(lane_in, 16), lax.div(lane_out, 16)

    def move(values, where):
        high = values.astype(BF16)
        rest = values - high.astype(F32)
        middle = rest.astype(BF16)
        low = (rest - middle.astype(F32)).astype(BF16)
        places = jnp.where(same_row & where, SCALE, 0.0).astype(BF16)
        moved = lax.dot_general(
            jnp.concatenate([high, middle, low], axis=0), places, (((1,), (0,)), ((), ())),
            preferred_element_type=F32,
        )
        count = values.shape[0]
        return moved[:count] + (moved[count : 2 * count] + moved[2 * count :])

    first0 = gain_sum[0].reshape(2, 2, 8, 128)
    for yh in range(2):
        rows0 = jnp.zeros((16, 128), F32)
        for xl in range(2):
            where = (group_in == yh * 4 + lax.div(group_out, 2)) & (lax.rem(group_out, 2) == xl)
            rows0 = rows0 + move(first0[:, xl].reshape(16, 128), where)
        for j in range(BLOCKS):
            gain_grad[4 * j + yh : 4 * j + yh + 1, :] = rows0[j : j + 1]
    z_of = lax.broadcasted_iota(jnp.int32, (8, 128), 0)
    z_lane = lax.div(lax.broadcasted_iota(jnp.int32, (8, 128), 1), 16)
    rows1 = jnp.zeros((32, 128), F32)
    for group in range(8):
        values = []
        for quarter in range(4):
            line = (quarter // 2) * 16 + (group % 2) * 8 + (quarter % 2) * 4 + group // 2
            one = jnp.broadcast_to(gain_sum[1, line : line + 1, :], (8, 128))
            values.append(jnp.where(z_of == z_lane, one, 0.0))
        rows1 = rows1 + move(jnp.concatenate(values, axis=0), group_out == group)
    for quarter in range(4):
        for z in range(8):
            row = 4 * ((quarter // 2) * 8 + z) + 2 + quarter % 2
            gain_grad[row : row + 1, :] = rows1[quarter * 8 + z : quarter * 8 + z + 1]
    for copy in wide_out:
        copy.wait()


def on_device(normed, norm_gain, kv_cot, master, moment1, moment2):
    width = normed.shape[1]
    vmem = pl.BlockSpec(memory_space=pltpu.VMEM)
    anywhere = pl.BlockSpec(memory_space=pl.ANY)
    owned = jax.ShapeDtypeStruct(master.shape, F32)
    wide = jax.ShapeDtypeStruct(normed.shape, BF16)
    gain = norm_gain.reshape(width // 128, 128)
    dma = pltpu.SemaphoreType.DMA
    grad_sum, gain_sum, normed_grad = pl.pallas_call(
        kernel,
        name="zero_backward",
        out_shape=(owned, jax.ShapeDtypeStruct((2, width // 256, 128), F32), wide),
        in_specs=[anywhere] * 4,
        out_specs=(vmem, vmem, anywhere),
        scratch_shapes=[
            pltpu.VMEM((width // 128, 128), F32),
            pltpu.VMEM(master.shape, F32),
            pltpu.VMEM(normed.shape, BF16),
            pltpu.VMEM((BLOCKS, 128, 256), BF16),
            pltpu.VMEM((2, 128, 256), BF16),
            pltpu.VMEM((2, 2, 8, 8, 2, 16, 128), BF16),
            pltpu.VMEM((2, 2, 8, 8, 2, 16, 128), BF16),
            pltpu.VMEM((2, 4, 8, 16, 128), BF16),
            pltpu.VMEM((2, 8, 8, 16, 128), BF16),
            pltpu.VMEM((8, 8, 16, 128), BF16),
            pltpu.VMEM((7, 8, 16, 128), BF16),
            pltpu.VMEM((8, 16, 128), BF16),
            pltpu.VMEM((7, 16, 128), BF16),
            pltpu.VMEM((2, 2, 8, 2, 16, 128), BF16),
            pltpu.VMEM((2, 8, 2, 16, 128), BF16),
            pltpu.VMEM((4, 2, 8, 2, 16, 128), BF16),
            pltpu.VMEM((2, 8, 2, 16, 128), BF16),
            pltpu.VMEM((3, 8, 16, 128), BF16),
            pltpu.VMEM((8, 16, 128), BF16),
            pltpu.VMEM((7, 16, 128), BF16),
            pltpu.VMEM((8, 32, 128), F32),
            pltpu.VMEM((8, 32, 128), F32),
            pltpu.VMEM((2, 4, 32, 128), F32),
            pltpu.VMEM((8, 8, 16, 128), F32),
            pltpu.VMEM((4, 8, 16, 128), F32),
            pltpu.VMEM((BLOCKS, 2, 128, 256), BF16),
            pltpu.VMEM((BLOCKS, 128, 256), BF16),
            pltpu.VMEM((128, 16, 128), BF16),
            pltpu.VMEM((16, 16, 128), F32),
            dma((2,)),
            dma((GROUPS,)),
            dma((GROUPS,)),
            dma((2,)),
            dma((LOADS + 1,)),
            dma((LOADS + 1,)),
            dma,
            dma((4,)),
            dma((2,)),
        ],
        compiler_params=pltpu.CompilerParams(
            collective_id=0, has_side_effects=True, vmem_limit_bytes=64 * 1024 * 1024
        ),
        cost_estimate=pl.CostEstimate(flops=1 << 30, bytes_accessed=4 << 20, transcendentals=4096),
    )(normed, gain, kv_cot, master)
    new_master, new_moment1, new_moment2, gain_grad, normed_grad = pl.pallas_call(
        finish,
        name="adamw",
        out_shape=(owned, owned, owned, jax.ShapeDtypeStruct(gain.shape, F32), wide),
        in_specs=[anywhere] * 7,
        out_specs=(vmem, vmem, vmem, vmem, anywhere),
        scratch_shapes=[
            pltpu.VMEM(master.shape, F32),
            pltpu.VMEM((2, width // 256, 128), F32),
            pltpu.VMEM(gain.shape, F32),
            pltpu.VMEM(master.shape, F32),
            pltpu.VMEM(master.shape, F32),
            pltpu.VMEM(master.shape, F32),
            pltpu.VMEM(normed.shape, BF16),
            dma((6,)),
            dma((2, CHUNKS)),
        ],
        compiler_params=pltpu.CompilerParams(vmem_limit_bytes=64 * 1024 * 1024),
    )(grad_sum, gain_sum, normed_grad, gain, master, moment1, moment2)
    return new_master, new_moment1, new_moment2, gain_grad.reshape(width), normed_grad


def solution(mesh):
    split = P(("row", "col"), None)
    return jax.shard_map(
        on_device,
        mesh=mesh,
        in_specs=(split, P(), split, split, split, split),
        out_specs=(split, split, split, P(), split),
        check_vma=False,
    )
```

```python
import math

import jax
import jax.numpy as jnp
from jax import lax
from jax.experimental import pallas as pl
from jax.experimental.pallas import tpu as pltpu
from jax.sharding import PartitionSpec as P

STEP = 100
TOTAL_TOKENS = 65536
SCALE = 1.0 / float(TOTAL_TOKENS) ** 0.5
MESH = pl.DeviceIdType.MESH
F32 = jnp.float32
BF16 = jnp.bfloat16

GROUPS = 26
BLOCKS = 16
CHUNKS = 8
LOADS = 4


def kernel(
    normed, gain_hbm, kv, master_hbm,
    grad_sum, gain_sum, normed_grad,
    gain, master,
    own, sib, kv2, w, g, qx, fx, s0, rb0, t0, ra0, qf, qh, fa, s1b, rx1, t1, rb1,
    ga, gb, gx, summed0, summed1, stage, inbox, yard, yard32,
    small, ssem, rsem, ex_send, ex_recv, ex_local, out_send, out_recv, out_local,
):
    r = lax.axis_index("row")
    c = lax.axis_index("col")
    core = lax.rem(r, 2)
    z = lax.rem(lax.div(r, 2), 8)
    xh = lax.div(r, 16)
    xl = lax.rem(c, 2)
    y = lax.div(c, 2)
    x = xh * 2 + xl
    a = z * (1 - core) + y * core
    b = y * (1 - core) + z * core

    def dev(xx, aa, bb, cc=None):
        zz = aa * (1 - core) + bb * core
        yy = bb * (1 - core) + aa * core
        cc = core if cc is None else cc
        return {"row": lax.div(xx, 2) * 16 + zz * 2 + cc, "col": yy * 2 + lax.rem(xx, 2)}

    sibling = dev(x, a, b, 1 - core)
    x_peer = [lax.rem(x + k, 4) for k in range(1, 4)]
    a_peer = [lax.rem(a + k, 8) for k in range(1, 8)]
    b_peer = [lax.rem(b + k, 8) for k in range(1, 8)]
    x_dev = [dev(v, a, b) for v in x_peer]
    a_dev = [dev(x, v, b) for v in a_peer]
    b_dev = [dev(x, a, v) for v in b_peer]

    def cols(j, cc):
        return pl.ds(pl.multiple_of(j * 512 + cc * 256, 256), 256)

    def remote(src, dst, send, recv, device):
        return pltpu.make_async_remote_copy(
            src_ref=src, dst_ref=dst, send_sem=send, recv_sem=recv,
            device_id=device, device_id_type=MESH,
        )

    def load_copy(k):
        part = pl.ds(pl.multiple_of(k * 2048, 2048), 2048)
        return pltpu.make_async_copy(normed.at[:, part], own.at[:, part], ex_local.at[k])

    def swap_copy(k, q):
        j = 4 * k + q
        return remote(own.at[:, cols(j, 1 - core)], sib.at[j], ex_send.at[0], ex_recv.at[k], sibling)

    def swap_wait(k):
        part = sib.at[pl.ds(4 * k, 4)]
        return remote(part, part, ex_send.at[0], ex_recv.at[k], sibling)

    kv_load = pltpu.make_async_copy(kv, kv2.at[0], ex_local.at[4])
    kv_swap = remote(kv2.at[0], kv2.at[1], ex_send.at[1], ex_recv.at[4], sibling)

    barrier = pltpu.get_barrier_semaphore()
    across_dev = [dev(v, a, b, 1 - core) for v in x_peer]
    partners = [sibling] + x_dev + across_dev + a_dev + b_dev
    for device in partners:
        pl.semaphore_signal(barrier, inc=1, device_id=device, device_id_type=MESH)

    master_load = pltpu.make_async_copy(master_hbm, master, small.at[0])
    gain_load = pltpu.make_async_copy(gain_hbm, gain, small.at[1])
    master_load.start()
    kv_load.start()

    @pl.loop(0, LOADS)
    def _(k):
        load_copy(k).start()

    gain_load.start()
    master_load.wait()
    w[0, xh, a, b, xl] = master[:, :128].astype(BF16)
    w[1, xh, a, b, xl] = master[:, 128:].astype(BF16)
    pl.semaphore_wait(barrier, len(partners))

    pending = []

    def group_wait(entry):
        number, tiles, dtype = entry
        counted = (yard if dtype == BF16 else yard32).at[pl.ds(0, tiles)]
        return remote(counted, counted, ssem.at[number], rsem.at[number], sibling)

    def exchange(copies):
        number = len(pending)
        tiles = 0
        for src, dst, device in copies:
            remote(src, dst, ssem.at[number], rsem.at[number], device).start()
            tiles += math.prod(src.shape) // (16 * 128)
        pending.append((number, tiles, src.dtype))
        return pending[-1]

    def arrive(entry):
        group_wait(entry).wait_recv()

    def spread(block, devices):
        return exchange([(block, block, device) for device in devices])

    def total(first, others):
        value = first.astype(F32)
        for other in others:
            value = value + other.astype(F32)
        return value

    def wrap(v, k, n):
        return lax.rem(v + k + n, n)

    xp, xm, xo = wrap(x, 1, 4), wrap(x, -1, 4), wrap(x, 2, 4)
    ap1, am1, ap2, am2 = (wrap(a, k, 8) for k in (1, -1, 2, -2))
    ap3, am3, ao = (wrap(a, k, 8) for k in (3, -3, 4))
    to_xp, to_xm = dev(xp, a, b), dev(xm, a, b)
    to_ap1, to_am1, to_ap2, to_am2 = (dev(x, v, b) for v in (ap1, am1, ap2, am2))
    low, high = pl.ds(0, 4), pl.ds(4, 4)

    def w_half(v, part):
        return w.at[0, lax.div(v, 2), part, :, lax.rem(v, 2)]

    def g_half(v, part):
        return g.at[0, lax.div(v, 2), part, :, lax.rem(v, 2)]

    st = {}

    def s1():
        st["ag0_a"] = spread(w.at[0, xh, a, b, xl], a_dev)
        st["ag1_b"] = spread(w.at[1, xh, a, b, xl], b_dev)

    def swap():
        kv_load.wait()
        kv_swap.start()

        @pl.loop(0, LOADS)
        def _(k):
            load_copy(k).wait()
            for q in range(4):
                swap_copy(k, q).start()

    def s2():
        arrive(st["ag0_a"])
        st["ag0_b"] = spread(w.at[0, xh, :, b, xl], b_dev)
        arrive(st["ag1_b"])
        st["ag1_x"] = spread(w.at[1, xh, a, :, xl], x_dev)

    def gp():
        kv_swap.wait_recv()

        @pl.loop(0, LOADS)
        def _(k):
            swap_wait(k).wait_recv()

            @pl.loop(0, 4)
            def _(q):
                j = 4 * k + q
                tokens = jnp.concatenate([own[:, cols(j, core)], sib[j]], axis=0)
                term = lax.dot_general(
                    tokens, kv2[...].reshape(256, 256), (((0,), (0,)), ((), ())),
                    preferred_element_type=F32,
                ).astype(BF16)
                bh = lax.div(j, 8)
                bz = lax.rem(j, 8)
                for i in range(8):
                    ia = bz * (1 - core) + i * core
                    ib = i * (1 - core) + bz * core
                    piece = term[32 * i : 32 * i + 32]
                    g[0, bh, ia, ib] = piece[:, :128].reshape(2, 16, 128)
                    g[1, bh, ia, ib] = piece[:, 128:].reshape(2, 16, 128)

    def s3():
        arrive(st["ag1_x"])
        plane = w.at[1, :, a]
        st["from_am2"] = spread(plane, [to_ap2])
        st["from_ap2"] = spread(plane, [to_am2])
        st["ag1_a"] = spread(plane, [to_ap1, to_am1])
        arrive(st["ag0_b"])
        st["from_xm"] = spread(w.at[0, xh, :, :, xl], [to_xp])
        st["from_xp"] = spread(w.at[0, xh, :, :, xl], [to_xm])

    def s3_on():
        arrive(st["from_am2"])
        far = w.at[1, :, am2]
        far_half = w.at[1, 1, am2]
        st["on_p"] = exchange([(far_half, far_half, to_ap2), (far, far, to_ap1)])
        arrive(st["from_ap2"])
        far = w.at[1, :, ap2]
        far_half = w.at[1, 0, ap2]
        st["on_m"] = exchange([(far_half, far_half, to_am2), (far, far, to_am1)])
        arrive(st["from_xm"])
        half = w_half(xm, low)
        st["on_xp"] = exchange([(half, half, to_xp)])
        arrive(st["from_xp"])
        half = w_half(xp, high)
        st["on_xm"] = exchange([(half, half, to_xm)])

    def s3_wait():
        arrive(st["ag1_a"])
        for name in ("on_p", "on_m", "on_xp", "on_xm"):
            arrive(st[name])

    def r1():
        st["r1_a"] = exchange([
                (g.at[1, 0, ao], qh.at[0], to_am2),
                (g.at[1, 1, ao], qh.at[1], to_ap2),
                (g.at[1, :, am3], qf.at[0], to_am1),
                (g.at[1, :, ap3], qf.at[1], to_ap1),
            ]
        )
        st["r1_a_near"] = exchange(
            [
                (g.at[1, :, ap1], fa.at[0], to_ap1),
                (g.at[1, :, am1], fa.at[1], to_am1),
            ],
        )
        st["r1_x"] = exchange([
                (g_half(xo, low), qx.at[0], to_xp),
                (g_half(xo, high), qx.at[1], to_xm),
            ]
        )
        st["r1_x_near"] = exchange(
            [
                (g_half(xp, high), fx.at[0, high], to_xp),
                (g_half(xm, low), fx.at[1, low], to_xm),
            ],
        )

    def r1_on():
        arrive(st["r1_a"])

        @pl.loop(0, 8)
        def _(i):
            g[1, 0, am2, i] = total(g[1, 0, am2, i], [qf[0, 0, i], qh[0, i]]).astype(BF16)
            g[1, 1, am2, i] = total(g[1, 1, am2, i], [qf[0, 1, i]]).astype(BF16)
            g[1, 0, ap2, i] = total(g[1, 0, ap2, i], [qf[1, 0, i]]).astype(BF16)
            g[1, 1, ap2, i] = total(g[1, 1, ap2, i], [qf[1, 1, i], qh[1, i]]).astype(BF16)

        st["r1_a_on"] = exchange([(g.at[1, :, am2], fa.at[2], to_am2), (g.at[1, :, ap2], fa.at[3], to_ap2)]
        )
        arrive(st["r1_x"])
        xph, xpl, xmh, xml = lax.div(xp, 2), lax.rem(xp, 2), lax.div(xm, 2), lax.rem(xm, 2)

        @pl.loop(0, 4)
        def _(i):
            g[0, xph, i, :, xpl] = total(g[0, xph, i, :, xpl], [qx[0, i]]).astype(BF16)
            g[0, xmh, 4 + i, :, xml] = total(g[0, xmh, 4 + i, :, xml], [qx[1, i]]).astype(BF16)

        st["r1_x_on"] = exchange([(g_half(xp, low), fx.at[0, low], to_xp), (g_half(xm, high), fx.at[1, high], to_xm)],
        )

    def out_copy(j):
        return pltpu.make_async_copy(
            stage.at[j, 0], normed_grad.at[:, cols(j, core)], out_local.at[0]
        )

    def out_swap(j):
        return remote(stage.at[j, 1], inbox.at[j], out_send, out_recv.at[lax.div(j, 4)], sibling)

    def in_copy(j):
        return pltpu.make_async_copy(
            inbox.at[j], normed_grad.at[:, cols(j, 1 - core)], out_local.at[1]
        )

    def mm():
        gain_load.wait()

        @pl.loop(0, BLOCKS)
        def _(j):
            bh = lax.div(j, 8)
            bz = lax.rem(j, 8)
            pieces = []
            for i in range(8):
                ia = bz * (1 - core) + i * core
                ib = i * (1 - core) + bz * core
                pieces.append(
                    jnp.concatenate(
                        [w[0, bh, ia, ib].reshape(32, 128), w[1, bh, ia, ib].reshape(32, 128)], axis=1
                    )
                )
            block = jnp.concatenate(pieces, axis=0)
            input_grad = lax.dot_general(
                kv2[...].reshape(256, 256), block, (((1,), (1,)), ((), ())), preferred_element_type=F32
            )
            row = 4 * j + 2 * core
            factor = jnp.concatenate([gain[pl.ds(row, 1), :], gain[pl.ds(row + 1, 1), :]], axis=1)
            stage[j] = (input_grad * factor).astype(BF16).reshape(2, 128, 256)
            out_copy(j).start()
            out_swap(j).start()

    shape3 = (8, 16, 128)
    diagonal = lax.broadcasted_iota(jnp.int32, shape3, 2) == (
        lax.broadcasted_iota(jnp.int32, shape3, 0) * 16 + lax.broadcasted_iota(jnp.int32, shape3, 1)
    )

    def contract(sums, weights):
        dots = jnp.sum(sums * weights.astype(F32), axis=2, keepdims=True)
        spread_out = jnp.where(diagonal, jnp.broadcast_to(dots, shape3), 0.0)
        return jnp.sum(jnp.sum(spread_out, axis=0), axis=0, keepdims=True)

    def gain_a():
        ga[a] = jnp.zeros((32, 128), F32)
        for i in range(8):
            ga[a, pl.ds(x * 8 + i, 1), :] = contract(summed0[i], w[0, xh, i, :, xl])
        for v in range(4):
            at = pl.ds(v * 8 + a, 1)
            ga[a, at, :] = ga[a, at, :] + contract(summed1[v], w[1, v // 2, a, :, v % 2])
        st["gain_a"] = spread(ga.at[a], a_dev)

    def gain_b():
        arrive(st["gain_a"])
        gb[b] = total(ga[0], [ga[k] for k in range(1, 8)])
        st["gain_b"] = spread(gb.at[b], b_dev)

    def gain_x():
        arrive(st["gain_b"])
        part = gx.at[core, x]
        part[...] = total(gb[0], [gb[k] for k in range(1, 8)])
        st["gain_x"] = spread(part, x_dev + across_dev + [sibling])

    def gain_end():
        arrive(st["gain_x"])
        for cc in range(2):
            gain_sum[cc] = total(gx[cc, 0], [gx[cc, k] for k in range(1, 4)])

    def r2():
        arrive(st["r1_a_near"])
        arrive(st["r1_a_on"])

        for h in range(2):
            for q in range(2):
                value = total(g[1, h, a, :, q], [fa[k, h, :, q] for k in range(4)])
                s1b[h, :, q] = value.astype(BF16)
                summed1[2 * h + q] = value

        st["r2_x"] = exchange([
                (s1b.at[lax.div(v, 2), :, lax.rem(v, 2)], rx1.at[k], x_dev[k])
                for k, v in enumerate(x_peer)
            ],
        )
        arrive(st["r1_x_near"])
        arrive(st["r1_x_on"])

        @pl.loop(0, 8)
        def _(i):
            value = total(g[0, xh, i, :, xl], [fx[k, i] for k in range(2)])
            s0[i] = value.astype(BF16)
            summed0[i] = value

        st["r2_b"] = exchange([(s0.at[:, v], rb0.at[k], b_dev[k]) for k, v in enumerate(b_peer)]
        )

    def r3():
        arrive(st["r2_x"])
        t1[...] = total(s1b[xh, :, xl], [rx1[k] for k in range(3)]).astype(BF16)
        st["r3_b"] = exchange([(t1.at[v], rb1.at[k], b_dev[k]) for k, v in enumerate(b_peer)]
        )
        arrive(st["r2_b"])
        t0[...] = total(s0[:, b], [rb0[k] for k in range(7)]).astype(BF16)
        st["r3_a"] = exchange([(t0.at[v], ra0.at[k], a_dev[k]) for k, v in enumerate(a_peer)]
        )

    def r_end():
        arrive(st["r3_b"])
        grad_sum[:, 128:] = total(t1[b], [rb1[k] for k in range(7)])
        arrive(st["r3_a"])
        grad_sum[:, :128] = total(t0[a], [ra0[k] for k in range(7)])

    def end():
        for entry in pending:
            group_wait(entry).wait_send()

    def end_swap():
        kv_swap.wait_send()
        remote(sib, sib, ex_send.at[0], ex_recv.at[0], sibling).wait_send()

    def pass_in():
        for k in range(4):
            part = inbox.at[pl.ds(4 * k, 4)]
            remote(part, part, out_send, out_recv.at[k], sibling).wait_recv()
            for q in range(4):
                in_copy(4 * k + q).start()

    def end_mm():
        remote(inbox, inbox, out_send, out_recv.at[0], sibling).wait_send()
        for k in range(2):
            pltpu.make_async_copy(inbox, inbox, out_local.at[k]).wait()

    for step in (
        s1, swap, gp, r1, s2, r1_on, s3, r2, gain_a, s3_on, gain_b, r3, gain_x, s3_wait, mm,
        pass_in, r_end, gain_end, end, end_swap, end_mm,
    ):
        step()


def finish(
    grad_hbm, gain_sum_hbm, normed_grad, gain_hbm, master_hbm, moment1_hbm, moment2_hbm,
    new_master, new_moment1, new_moment2, gain_grad, normed_grad_out,
    grad_sum, gain_sum, gain, master, moment1, moment2, wide, sem, wide_sem,
):
    rows = normed_grad.shape[0] // CHUNKS
    parts = [pl.ds(rows * k, rows) for k in range(CHUNKS)]
    wide_in = [
        pltpu.make_async_copy(normed_grad.at[part], wide.at[part], wide_sem.at[0, k])
        for k, part in enumerate(parts)
    ]
    wide_out = [
        pltpu.make_async_copy(wide.at[part], normed_grad_out.at[part], wide_sem.at[1, k])
        for k, part in enumerate(parts)
    ]
    pairs = (
        (grad_hbm, grad_sum), (gain_sum_hbm, gain_sum), (gain_hbm, gain),
        (master_hbm, master), (moment1_hbm, moment1), (moment2_hbm, moment2),
    )
    loads = [pltpu.make_async_copy(src, dst, sem.at[k]) for k, (src, dst) in enumerate(pairs)]
    for copy in loads + wide_in:
        copy.start()
    def pass_on(first, last):
        for into, out in zip(wide_in[first:last], wide_out[first:last]):
            into.wait()
            out.start()

    for copy in loads:
        copy.wait()
    p = lax.axis_index("row") * 16 + lax.axis_index("col")
    own_gain = jnp.broadcast_to(gain[pl.ds(lax.div(p, 8), 1), :], (16, 128))
    lane = lax.broadcasted_iota(jnp.int32, (16, 128), 1)
    sub = lax.broadcasted_iota(jnp.int32, (16, 128), 0)
    factor = jnp.sum(
        jnp.where(lane == sub + lax.rem(p, 8) * 16, own_gain, 0.0), axis=1, keepdims=True
    )
    grad = grad_sum[...] * (factor * SCALE)
    m1 = 0.9 * moment1[...] + 0.1 * grad
    m2 = 0.95 * moment2[...] + 0.05 * grad * grad
    new_moment1[...] = m1
    new_moment2[...] = m2
    first = m1 / (1.0 - 0.9**STEP)
    second = m2 / (1.0 - 0.95**STEP)
    new_master[...] = master[...] - 0.01 * (first / (jnp.sqrt(second) + 1e-08) + 0.1 * master[...])
    pass_on(0, CHUNKS)
    lane_in = lax.broadcasted_iota(jnp.int32, (128, 128), 0)
    lane_out = lax.broadcasted_iota(jnp.int32, (128, 128), 1)
    same_row = lax.rem(lane_in, 16) == lax.rem(lane_out, 16)
    group_in, group_out = lax.div(lane_in, 16), lax.div(lane_out, 16)

    def move(values, where):
        high = values.astype(BF16)
        rest = values - high.astype(F32)
        middle = rest.astype(BF16)
        low = (rest - middle.astype(F32)).astype(BF16)
        places = jnp.where(same_row & where, SCALE, 0.0).astype(BF16)
        moved = lax.dot_general(
            jnp.concatenate([high, middle, low], axis=0), places, (((1,), (0,)), ((), ())),
            preferred_element_type=F32,
        )
        count = values.shape[0]
        return moved[:count] + (moved[count : 2 * count] + moved[2 * count :])

    first0 = gain_sum[0].reshape(2, 2, 8, 128)
    for yh in range(2):
        rows0 = jnp.zeros((16, 128), F32)
        for xl in range(2):
            where = (group_in == yh * 4 + lax.div(group_out, 2)) & (lax.rem(group_out, 2) == xl)
            rows0 = rows0 + move(first0[:, xl].reshape(16, 128), where)
        for j in range(BLOCKS):
            gain_grad[4 * j + yh : 4 * j + yh + 1, :] = rows0[j : j + 1]
    z_of = lax.broadcasted_iota(jnp.int32, (8, 128), 0)
    z_lane = lax.div(lax.broadcasted_iota(jnp.int32, (8, 128), 1), 16)
    rows1 = jnp.zeros((32, 128), F32)
    for group in range(8):
        values = []
        for quarter in range(4):
            line = (quarter // 2) * 16 + (group % 2) * 8 + (quarter % 2) * 4 + group // 2
            one = jnp.broadcast_to(gain_sum[1, line : line + 1, :], (8, 128))
            values.append(jnp.where(z_of == z_lane, one, 0.0))
        rows1 = rows1 + move(jnp.concatenate(values, axis=0), group_out == group)
    for quarter in range(4):
        for z in range(8):
            row = 4 * ((quarter // 2) * 8 + z) + 2 + quarter % 2
            gain_grad[row : row + 1, :] = rows1[quarter * 8 + z : quarter * 8 + z + 1]
    for copy in wide_out:
        copy.wait()


def on_device(normed, norm_gain, kv_cot, master, moment1, moment2):
    width = normed.shape[1]
    vmem = pl.BlockSpec(memory_space=pltpu.VMEM)
    anywhere = pl.BlockSpec(memory_space=pl.ANY)
    owned = jax.ShapeDtypeStruct(master.shape, F32)
    wide = jax.ShapeDtypeStruct(normed.shape, BF16)
    gain = norm_gain.reshape(width // 128, 128)
    dma = pltpu.SemaphoreType.DMA
    grad_sum, gain_sum, normed_grad = pl.pallas_call(
        kernel,
        name="zero_backward",
        out_shape=(owned, jax.ShapeDtypeStruct((2, width // 256, 128), F32), wide),
        in_specs=[anywhere] * 4,
        out_specs=(vmem, vmem, anywhere),
        scratch_shapes=[
            pltpu.VMEM((width // 128, 128), F32),
            pltpu.VMEM(master.shape, F32),
            pltpu.VMEM(normed.shape, BF16),
            pltpu.VMEM((BLOCKS, 128, 256), BF16),
            pltpu.VMEM((2, 128, 256), BF16),
            pltpu.VMEM((2, 2, 8, 8, 2, 16, 128), BF16),
            pltpu.VMEM((2, 2, 8, 8, 2, 16, 128), BF16),
            pltpu.VMEM((2, 4, 8, 16, 128), BF16),
            pltpu.VMEM((2, 8, 8, 16, 128), BF16),
            pltpu.VMEM((8, 8, 16, 128), BF16),
            pltpu.VMEM((7, 8, 16, 128), BF16),
            pltpu.VMEM((8, 16, 128), BF16),
            pltpu.VMEM((7, 16, 128), BF16),
            pltpu.VMEM((2, 2, 8, 2, 16, 128), BF16),
            pltpu.VMEM((2, 8, 2, 16, 128), BF16),
            pltpu.VMEM((4, 2, 8, 2, 16, 128), BF16),
            pltpu.VMEM((2, 8, 2, 16, 128), BF16),
            pltpu.VMEM((3, 8, 16, 128), BF16),
            pltpu.VMEM((8, 16, 128), BF16),
            pltpu.VMEM((7, 16, 128), BF16),
            pltpu.VMEM((8, 32, 128), F32),
            pltpu.VMEM((8, 32, 128), F32),
            pltpu.VMEM((2, 4, 32, 128), F32),
            pltpu.VMEM((8, 8, 16, 128), F32),
            pltpu.VMEM((4, 8, 16, 128), F32),
            pltpu.VMEM((BLOCKS, 2, 128, 256), BF16),
            pltpu.VMEM((BLOCKS, 128, 256), BF16),
            pltpu.VMEM((128, 16, 128), BF16),
            pltpu.VMEM((16, 16, 128), F32),
            dma((2,)),
            dma((GROUPS,)),
            dma((GROUPS,)),
            dma((2,)),
            dma((LOADS + 1,)),
            dma((LOADS + 1,)),
            dma,
            dma((4,)),
            dma((2,)),
        ],
        compiler_params=pltpu.CompilerParams(
            collective_id=0, has_side_effects=True, vmem_limit_bytes=64 * 1024 * 1024
        ),
        cost_estimate=pl.CostEstimate(flops=1 << 30, bytes_accessed=4 << 20, transcendentals=4096),
    )(normed, gain, kv_cot, master)
    new_master, new_moment1, new_moment2, gain_grad, normed_grad = pl.pallas_call(
        finish,
        name="adamw",
        out_shape=(owned, owned, owned, jax.ShapeDtypeStruct(gain.shape, F32), wide),
        in_specs=[anywhere] * 7,
        out_specs=(vmem, vmem, vmem, vmem, anywhere),
        scratch_shapes=[
            pltpu.VMEM(master.shape, F32),
            pltpu.VMEM((2, width // 256, 128), F32),
            pltpu.VMEM(gain.shape, F32),
            pltpu.VMEM(master.shape, F32),
            pltpu.VMEM(master.shape, F32),
            pltpu.VMEM(master.shape, F32),
            pltpu.VMEM(normed.shape, BF16),
            dma((6,)),
            dma((2, CHUNKS)),
        ],
        compiler_params=pltpu.CompilerParams(vmem_limit_bytes=64 * 1024 * 1024),
    )(grad_sum, gain_sum, normed_grad, gain, master, moment1, moment2)
    return new_master, new_moment1, new_moment2, gain_grad.reshape(width), normed_grad


def solution(mesh):
    split = P(("row", "col"), None)
    return jax.shard_map(
        on_device,
        mesh=mesh,
        in_specs=(split, P(), split, split, split, split),
        out_specs=(split, split, split, P(), split),
        check_vma=False,
    )
```
